128 devices in a mesh: lat: 64 (over x, z, y_lo, core), lon: 2 (over y_hi).
Axes of the slice: x: 4, y: 4 (y_hi: 2, y_lo: 2; y = y_hi * 2 + y_lo), z: 4, core: 2. Of those that a mesh axis runs over, the one named last changes fastest.
Arguments:
- grid_field: bfloat16 [384, 1440, 512], P('lat', 'lon'), may hold values from -6 to 6
- disco_taps: float32 [3, 384, 3, 5], P(None, 'lat'), may hold values from -1.5 to 1.5
- disco_mix: bfloat16 [1536, 512], replicated, may hold values from -0.15625 to 0.15625
- legendre: bfloat16 [256, 256, 384], P('lat'), may hold values from -0.3125 to 0.3125
- quad_weights: float32 [384], P('lat'), may hold values from 0.5 to 2
- mix_weight: bfloat16 [2, 512, 512], replicated, may hold values from -0.1875 to 0.1875
- degree_gain: float32 [256, 512], replicated, may hold values from 0.5 to 2
Outputs:
- block_output: bfloat16 [384, 1440, 512], P('lat', 'lon')
The draws below stay inside these ranges and needn't reach their ends.
All inputs are finite; a program needn't handle non-finite values.
Results may differ from the reference program's by a relative error of at most 0.018.
Values may be sent and summed in bfloat16 or wider, within the bound.
A program may use at most 320 MiB of HBM per device.

```python
import math
import jax
import jax.numpy as jnp
from jax import lax

C = 512
NLON = 1440
MODES = 256
DEGREES = 256
KERNELS = 3
LAT_DEV = 6
LAT = 384


def block_levels(own_key, extent, cuts, smallest, largest):
    level, own = 1.0, jax.random.fold_in(own_key, 6)
    for dim, blocks in cuts:
        heights = jnp.exp(jax.random.uniform(jax.random.fold_in(own, dim), (blocks,), jnp.float32, smallest / len(cuts), largest / len(cuts)))
        level = level * jnp.repeat(heights, extent[dim] // blocks).reshape([-1 if axis == dim else 1 for axis in range(len(extent))])
    return level


def centred(rng, extent, scale, bound, shards=(), kind=jnp.bfloat16):
    factor_of = block_levels(rng, extent, shards, -0.22, 0.18) if shards else 1.0
    result = jax.random.normal(rng, extent, jnp.float32) * scale * factor_of
    return jnp.minimum(jnp.maximum(result, -bound), bound).astype(kind)


def setup_inputs(seed: int = 0) -> dict:
    key_of = jax.random.split(jax.random.key(seed), 8)
    return {
        "grid_field": centred(key_of[0], (LAT, NLON, C), 1.0, 6.0, ((0, 64), (1, 2))),
        "disco_taps": centred(key_of[1], (KERNELS, LAT, 3, 5), 15 ** -0.5, 1.5, ((1, 64),), jnp.float32),
        "disco_mix": centred(key_of[2], (KERNELS * C, C), (KERNELS * C) ** -0.5, 0.15625),
        "legendre": centred(key_of[3], (MODES, DEGREES, LAT), LAT ** -0.5, 0.3125, ((0, 64),)),
        "quad_weights": jnp.clip(jnp.exp(math.log(2.0) - 1.3862944 * jax.random.uniform(key_of[4], (LAT,), jnp.float32) ** block_levels(key_of[4], (LAT,), ((0, 64),), -0.2, 0.2)), 0.5, 2.0),
        "mix_weight": centred(key_of[5], (2, C, C), (2 * C) ** -0.5, 0.1875),
        "degree_gain": jnp.clip(jnp.exp(jax.random.uniform(key_of[6], (DEGREES, C), jnp.float32, math.log(0.5), math.log(2.0))), 0.5, 2.0),
    }


def dft_basis(offset, number, length, mode_count):
    longitudes = offset + jnp.arange(number, dtype=jnp.int32)
    orders = jnp.arange(mode_count, dtype=jnp.int32)
    product = longitudes[:, None] * orders[None, :] % length
    angles = product.astype(jnp.float32) * (2.0 * math.pi / length)
    paired = jnp.stack([jnp.cos(angles), -jnp.sin(angles)], axis=2) * (1.0 / math.sqrt(length))
    return paired.reshape(number, 2 * mode_count).astype(jnp.bfloat16)

def triangle_table(legendre, first_mode):
    mode_count = legendre.shape[0]
    degree_count = legendre.shape[1]
    orders = first_mode + jnp.arange(mode_count, dtype=jnp.int32)
    degrees = jnp.arange(degree_count, dtype=jnp.int32)
    keep = degrees[None, :, None] >= orders[:, None, None]
    return jnp.where(keep, legendre, jnp.zeros_like(legendre))

def mixing_matrix(real_part, imag_part):
    upper = jnp.concatenate([real_part, imag_part], axis=1)
    lower = jnp.concatenate([-imag_part, real_part], axis=1)
    return jnp.concatenate([upper, lower], axis=0)

def reference(grid_field, disco_taps, disco_mix, legendre, quad_weights, mix_weight, degree_gain):
    lat_count, lon_count, channels = grid_field.shape
    kernels = disco_taps.shape[0]
    widened = jnp.concatenate([grid_field[:, -2:], grid_field, grid_field[:, :2]], axis=1)
    zero_cycle = jnp.zeros((1, lon_count + 4, channels), grid_field.dtype)
    padded = jnp.concatenate([zero_cycle, widened, zero_cycle], axis=0)
    basis_table = dft_basis(0, lon_count, lon_count, MODES).astype(jnp.float32)
    conv_weight = disco_mix.reshape(kernels, channels, channels).astype(jnp.float32)
    cycle_block = LAT_DEV

    def forward_block(first_row):
        rim_rows = lax.dynamic_slice_in_dim(padded, first_row, cycle_block + 2, 0)
        tap_block = lax.dynamic_slice_in_dim(disco_taps, first_row, cycle_block, 1)
        summed = jnp.zeros((kernels, cycle_block, lon_count, channels), jnp.float32)
        for row_shift in range(3):
            for col_shift in range(5):
                shifted = rim_rows[row_shift:row_shift + cycle_block, col_shift:col_shift + lon_count, :].astype(jnp.float32)
                summed = summed + tap_block[:, :, row_shift, col_shift][:, :, None, None] * shifted[None]
        basis_terms = lax.optimization_barrier(summed.astype(jnp.bfloat16))
        conv = jnp.einsum('kijc,kco->ijo', basis_terms.astype(jnp.float32), conv_weight)
        conv = lax.optimization_barrier(conv.astype(jnp.bfloat16))
        spectrum = jnp.einsum('jq,ijc->iqc', basis_table, conv.astype(jnp.float32))
        cycle_weights = lax.dynamic_slice_in_dim(quad_weights, first_row, cycle_block, 0)
        return (conv, (spectrum * cycle_weights[:, None, None]).astype(jnp.bfloat16))
    first_rows = jnp.arange(lat_count // cycle_block, dtype=jnp.int32) * cycle_block
    conv_blocks, spectra = lax.map(forward_block, first_rows)
    conv_all = lax.optimization_barrier(conv_blocks.reshape(lat_count, lon_count, channels))
    weighted = lax.optimization_barrier(spectra.reshape(lat_count, 2 * MODES, channels))
    triangle = triangle_table(legendre, 0).astype(jnp.float32)
    split_parts = weighted.astype(jnp.float32).reshape(lat_count, MODES, 2, channels)
    coeffs = jnp.einsum('mli,impc->mlpc', triangle, split_parts).astype(jnp.bfloat16)
    coeffs = lax.optimization_barrier(coeffs)
    block_weight = mixing_matrix(mix_weight[0], mix_weight[1])
    flattened = coeffs.reshape(MODES * DEGREES, 2 * channels)
    mixed_sum = jnp.dot(flattened, block_weight, preferred_element_type=jnp.float32).reshape(MODES, DEGREES, 2, channels)
    mixed_modes = lax.optimization_barrier((mixed_sum * degree_gain[None, :, None, :]).astype(jnp.bfloat16))
    synth = jnp.einsum('mli,mlpc->impc', triangle, mixed_modes.astype(jnp.float32)).astype(jnp.bfloat16)
    synth = lax.optimization_barrier(synth).reshape(lat_count, 2 * MODES, channels)

    def inverse_block(first_row):
        cycle_data = lax.dynamic_slice_in_dim(synth, first_row, cycle_block, 0).astype(jnp.float32)
        conv_rows = lax.dynamic_slice_in_dim(conv_all, first_row, cycle_block, 0).astype(jnp.float32)
        returned = jnp.einsum('jq,iqc->ijc', basis_table, cycle_data)
        return (conv_rows + returned).astype(jnp.bfloat16)
    output_blocks = lax.map(inverse_block, first_rows)
    return output_blocks.reshape(lat_count, lon_count, channels)
```

```python
import functools
import math

import jax
import jax.numpy as jnp
import numpy as np
from jax import lax
from jax.experimental import pallas as pl
from jax.experimental.pallas import tpu as pltpu
from jax.sharding import PartitionSpec as P

MESH = pl.DeviceIdType.MESH
C = 512
NLON = 1440
MODES = 256
DEGREES = 256
KERNELS = 3
CYCLES = 6
LATS = 64
LONS = 2
DEVS = LATS * LONS
HALF = NLON // LONS
EDGE = 16
WIDE = HALF + 2 * EDGE
TILE = 48
WINDOW = TILE + 2 * EDGE
PAIRS = ((1, 2), (3, 4), (0, 5))
F32, BF16 = jnp.float32, jnp.bfloat16


def dft_constants():
    j = np.arange(NLON, dtype=np.int64)[:, None]
    m = np.arange(MODES, dtype=np.int64)[None, :]
    angle = ((j * m) % NLON).astype(np.float64) * (2.0 * math.pi / NLON)
    pair = np.stack([np.cos(angle), -np.sin(angle)], axis=2) / math.sqrt(NLON)
    table = pair.reshape(LONS, HALF, 2 * MODES).astype(np.float32)
    forward = np.ascontiguousarray(table.transpose(0, 2, 1))
    return jnp.asarray(forward, BF16), jnp.asarray(table, BF16)


def dot(a, b):
    return jnp.dot(a, b, preferred_element_type=F32)


def build_taps(i, taps, band):
    rows = lax.broadcasted_iota(jnp.int32, (TILE, 3 * WINDOW), 0)
    cols = lax.broadcasted_iota(jnp.int32, (TILE, 3 * WINDOW), 1)
    shift = cols - rows
    for k in range(KERNELS):
        total = jnp.zeros((TILE, 3 * WINDOW), F32)
        for a in range(3):
            for b in range(5):
                value = taps[((k * CYCLES + i) * 3 + a) * 5 + b]
                total = jnp.where(shift == a * WINDOW + EDGE - 2 + b, value, total)
        band[k * TILE : (k + 1) * TILE, :] = total.astype(BF16)


def conv_cycle(i, taps, padded, band, terms, mix, conv):
    build_taps(i, taps, band)

    @pl.loop(0, HALF // TILE)
    def _(t):
        start = pl.multiple_of(t * TILE, 16)
        window = padded[pl.ds(i, 3), pl.ds(start, WINDOW), :].reshape(3 * WINDOW, C)
        basis = dot(band[...], window).astype(BF16)
        for k in range(KERNELS):
            terms[pl.ds(start, TILE), k * C : (k + 1) * C] = basis[k * TILE : (k + 1) * TILE]

    @pl.loop(0, 3)
    def _(t):
        rows = pl.ds(pl.multiple_of(t * 240, 16), 240)
        conv[i, rows, :] = dot(terms[rows, :], mix[...]).astype(BF16)


def dft_pair(p, cycles, quad, forward, conv, spectra, send):
    for s in range(2):

        @pl.loop(0, 2)
        def _(t):
            rows = pl.ds(pl.multiple_of(t * 256, 16), 256)
            spectra[s, rows, :] = dot(forward[rows, :], conv[cycles[s]]) * quad[cycles[s]]

    @pl.loop(0, 8)
    def _(t):
        rows = pl.ds(pl.multiple_of(t * 64, 16), 64)
        first = spectra[0, rows, :].reshape(8, 8, C)
        second = spectra[1, rows, :].reshape(8, 8, C)
        low = lax.broadcasted_iota(jnp.int32, (8, 8, C), 1) < 4
        even = jnp.where(low, first, pltpu.roll(second, 4, 1))
        odd = jnp.where(low, pltpu.roll(first, 4, 1), second)
        both = jnp.stack([even, odd], axis=1).reshape(16, 8, C)
        send[pl.ds(t * 16, 16), p] = both.astype(BF16)


def spread(p, columns_first):
    shape = (LATS * CYCLES, LATS * 8)
    cycle = lax.broadcasted_iota(jnp.int32, shape, 0)
    col = lax.broadcasted_iota(jnp.int32, shape, 1)
    place = (col // 4) % 2
    within = jnp.where(place == 0, PAIRS[p][0], PAIRS[p][1])
    return jnp.where(cycle == (col // 8) * CYCLES + within, 1.0, 0.0).astype(BF16)


def build_triangle(first_order, legendre, ones, table, turned):
    degree = lax.broadcasted_iota(jnp.int32, (DEGREES, LATS * CYCLES), 0)
    for m in range(2):
        values = legendre[m]
        legendre[m] = jnp.where(degree >= first_order + m, values.astype(F32), 0.0).astype(BF16)
    for p in range(3):
        ones[...] = spread(p, False)
        for m in range(2):
            wide = dot(legendre[m], ones[...])
            col = lax.broadcasted_iota(jnp.int32, wide.shape, 1) % 4
            tall = lax.dot_general(
                ones[...], legendre[m], (((0,), (1,)), ((), ())), preferred_element_type=F32
            )
            row = lax.broadcasted_iota(jnp.int32, tall.shape, 0) % 4
            for c in range(2):
                block = slice((2 * m + c) * DEGREES, (2 * m + c + 1) * DEGREES)
                table[p, block, :] = jnp.where(col == 2 * m + c, wide, 0.0).astype(BF16)
                turned[p, :, block] = jnp.where(row == 2 * m + c, tall, 0.0).astype(BF16)


def legendre_pair(p, received, joined, table, coeffs):
    @pl.loop(0, 8)
    def _(t):
        block = received[pl.ds(t * 16, 16), p].astype(F32).reshape(8, 2, 8, C)
        total = (block[:, 0] + block[:, 1]).reshape(64, C)
        joined[pl.ds(pl.multiple_of(t * 64, 16), 64), :] = total.astype(BF16)

    @pl.loop(0, 4)
    def _(t):
        rows = pl.ds(pl.multiple_of(t * 256, 16), 256)
        value = dot(table[p, rows, :], joined[...])
        if p == 0:
            coeffs[rows, :] = value
        else:
            coeffs[rows, :] += value


def mix_modes(coeffs, weight, gain, mixed):
    for m in range(2):
        real = coeffs[2 * m * DEGREES : (2 * m + 1) * DEGREES, :].astype(BF16)
        imag = coeffs[(2 * m + 1) * DEGREES : (2 * m + 2) * DEGREES, :].astype(BF16)
        new_real = (dot(real, weight[0]) - dot(imag, weight[1])) * gain[...]
        mixed[2 * m * DEGREES : (2 * m + 1) * DEGREES, :] = new_real.astype(BF16)
        new_imag = (dot(real, weight[1]) + dot(imag, weight[0])) * gain[...]
        mixed[(2 * m + 1) * DEGREES : (2 * m + 2) * DEGREES, :] = new_imag.astype(BF16)


def synth_pair(p, turned, mixed, send):
    @pl.loop(0, 4)
    def _(t):
        rows = pl.ds(pl.multiple_of(t * 128, 16), 128)
        value = dot(turned[p, rows, :], mixed[...]).astype(BF16).reshape(16, 8, C)
        send[pl.ds(t * 16, 16), p] = value


def inverse_pair(p, cycles, inverse, received, synth, conv, out):
    @pl.loop(0, 8)
    def _(t):
        block = received[pl.ds(t * 16, 16), p].astype(F32).reshape(8, 2, 8, C)
        first, second = block[:, 0], block[:, 1]
        low = lax.broadcasted_iota(jnp.int32, (8, 8, C), 1) < 4
        rows = pl.ds(pl.multiple_of(t * 64, 16), 64)
        even = jnp.where(low, first, pltpu.roll(second, 4, 1))
        odd = jnp.where(low, pltpu.roll(first, 4, 1), second)
        synth[0, rows, :] = even.reshape(64, C).astype(BF16)
        synth[1, rows, :] = odd.reshape(64, C).astype(BF16)

    for s in range(2):

        @pl.loop(0, 3)
        def _(t):
            rows = pl.ds(pl.multiple_of(t * 240, 16), 240)
            value = dot(inverse[rows, :], synth[s]) + conv[cycles[s], rows, :].astype(F32)
            out[cycles[s], rows, :] = value.astype(BF16)


def halo_copies(field, padded, send_sems, recv_sems):
    lat, lon = lax.axis_index("lat"), lax.axis_index("lon")
    up, down, other = (lat + LATS - 1) % LATS, (lat + 1) % LATS, 1 - lon
    head, body, tail = pl.ds(0, EDGE), pl.ds(EDGE, HALF), pl.ds(EDGE + HALF, EDGE)
    last = pl.ds(HALF - EDGE, EDGE)
    inner = pl.ds(1, CYCLES)
    plan = (
        (field.at[:, last], padded.at[inner, head], (lat, other)),
        (field.at[:, head], padded.at[inner, tail], (lat, other)),
        (field.at[0], padded.at[CYCLES + 1, body], (up, lon)),
        (field.at[CYCLES - 1], padded.at[0, body], (down, lon)),
        (field.at[0, last], padded.at[CYCLES + 1, head], (up, other)),
        (field.at[0, head], padded.at[CYCLES + 1, tail], (up, other)),
        (field.at[CYCLES - 1, last], padded.at[0, head], (down, other)),
        (field.at[CYCLES - 1, head], padded.at[0, tail], (down, other)),
    )
    return [
        pltpu.make_async_remote_copy(
            src_ref=src,
            dst_ref=dst,
            send_sem=send_sems.at[n],
            recv_sem=recv_sems.at[n],
            device_id=target,
            device_id_type=MESH,
        )
        for n, (src, dst, target) in enumerate(plan)
    ]


def forward_kernel(
    taps, quad, field, mix, forward_all, conv, send,
    padded, band, terms, forward, spectra, local_sems, send_sems, recv_sems,
):
    lat, lon = lax.axis_index("lat"), lax.axis_index("lon")
    load = pltpu.make_async_copy(field, padded.at[pl.ds(1, CYCLES), pl.ds(EDGE, HALF)], local_sems.at[0])
    load.start()
    table = pltpu.make_async_copy(forward_all.at[lon], forward, local_sems.at[1])
    table.start()
    barrier = pltpu.get_barrier_semaphore()
    up, down = (lat + LATS - 1) % LATS, (lat + 1) % LATS
    for peer in ((lat, 1 - lon), (up, lon), (down, lon), (up, 1 - lon), (down, 1 - lon)):
        pl.semaphore_signal(barrier, inc=1, device_id=peer, device_id_type=MESH)
    pl.semaphore_wait(barrier, 5)
    copies = halo_copies(field, padded, send_sems, recv_sems)
    for copy in copies:
        copy.start()
    load.wait()
    copies[0].wait_recv()
    copies[1].wait_recv()
    table.wait()
    for p, cycles in enumerate(PAIRS):
        if p == 2:
            for copy in copies[2:]:
                copy.wait_recv()

            @pl.when(lat == 0)
            def _():
                padded[0] = jnp.zeros((WIDE, C), BF16)

            @pl.when(lat == LATS - 1)
            def _():
                padded[CYCLES + 1] = jnp.zeros((WIDE, C), BF16)

        for i in cycles:
            conv_cycle(i, taps, padded, band, terms, mix, conv)
        dft_pair(p, cycles, quad, forward, conv, spectra, send)
    for copy in copies:
        copy.wait_send()


def middle_kernel(
    received, legendre_all, weight, gain, send, legendre, ones, table, turned, joined, coeffs, mixed, sems
):
    lat, lon = lax.axis_index("lat"), lax.axis_index("lon")
    load = pltpu.make_async_copy(legendre_all.at[pl.ds(2 * lon, 2)], legendre, sems.at[0])
    load.start()
    load.wait()
    build_triangle(4 * lat + 2 * lon, legendre, ones, table, turned)
    for p in range(3):
        legendre_pair(p, received, joined, table, coeffs)
    mix_modes(coeffs, weight, gain, mixed)
    for p in range(3):
        synth_pair(p, turned, mixed, send)


def inverse_kernel(received, conv, inverse_all, out, inverse, synth, sems):
    lon = lax.axis_index("lon")
    load = pltpu.make_async_copy(inverse_all.at[lon], inverse, sems.at[0])
    load.start()
    load.wait()
    for p, cycles in enumerate(PAIRS):
        inverse_pair(p, cycles, inverse, received, synth, conv, out)


VMEM = pl.BlockSpec(memory_space=pltpu.VMEM)
SMEM = pl.BlockSpec(memory_space=pltpu.SMEM)
ANY = pl.BlockSpec(memory_space=pl.ANY)
LIMIT = 56 * 2**20


def body(grid_field, disco_taps, disco_mix, legendre, quad_weights, mix_weight, degree_gain):
    forward_all, inverse_all = dft_constants()
    conv, send = pl.pallas_call(
        forward_kernel,
        out_shape=(
            jax.ShapeDtypeStruct((CYCLES, HALF, C), BF16),
            jax.ShapeDtypeStruct((DEVS, 3, 8, C), BF16),
        ),
        in_specs=[SMEM, SMEM, ANY, VMEM, ANY],
        out_specs=(VMEM, VMEM),
        scratch_shapes=[
            pltpu.VMEM((CYCLES + 2, WIDE, C), BF16),
            pltpu.VMEM((KERNELS * TILE, 3 * WINDOW), BF16),
            pltpu.VMEM((HALF, KERNELS * C), BF16),
            pltpu.VMEM((2 * MODES, HALF), BF16),
            pltpu.VMEM((2, 2 * MODES, C), F32),
            pltpu.SemaphoreType.DMA((2,)),
            pltpu.SemaphoreType.DMA((8,)),
            pltpu.SemaphoreType.DMA((8,)),
        ],
        compiler_params=pltpu.CompilerParams(
            collective_id=0, has_side_effects=True, vmem_limit_bytes=LIMIT
        ),
    )(disco_taps.reshape(-1), quad_weights, grid_field, disco_mix, forward_all)
    received = lax.all_to_all(send, ("lat", "lon"), split_axis=0, concat_axis=0, tiled=True)
    synth = pl.pallas_call(
        middle_kernel,
        out_shape=jax.ShapeDtypeStruct((LATS, 3, 8, C), BF16),
        in_specs=[VMEM, ANY, VMEM, VMEM],
        out_specs=VMEM,
        scratch_shapes=[
            pltpu.VMEM((2, DEGREES, LATS * CYCLES), BF16),
            pltpu.VMEM((LATS * CYCLES, LATS * 8), BF16),
            pltpu.VMEM((3, 4 * DEGREES, LATS * 8), BF16),
            pltpu.VMEM((3, LATS * 8, 4 * DEGREES), BF16),
            pltpu.VMEM((LATS * 8, C), BF16),
            pltpu.VMEM((4 * DEGREES, C), F32),
            pltpu.VMEM((4 * DEGREES, C), BF16),
            pltpu.SemaphoreType.DMA((1,)),
        ],
        compiler_params=pltpu.CompilerParams(vmem_limit_bytes=LIMIT),
    )(received, legendre, mix_weight, degree_gain)
    doubled = jnp.broadcast_to(synth[:, None], (LATS, 2, 3, 8, C)).reshape(DEVS, 3, 8, C)
    returned = lax.all_to_all(doubled, ("lat", "lon"), split_axis=0, concat_axis=0, tiled=True)
    return pl.pallas_call(
        inverse_kernel,
        out_shape=jax.ShapeDtypeStruct((CYCLES, HALF, C), BF16),
        in_specs=[VMEM, VMEM, ANY],
        out_specs=VMEM,
        scratch_shapes=[
            pltpu.VMEM((HALF, 2 * MODES), BF16),
            pltpu.VMEM((2, 2 * MODES, C), BF16),
            pltpu.SemaphoreType.DMA((1,)),
        ],
        compiler_params=pltpu.CompilerParams(vmem_limit_bytes=LIMIT),
    )(returned, conv, inverse_all)


def solution(mesh):
    return jax.shard_map(
        body,
        mesh=mesh,
        in_specs=(
            P("lat", "lon", None),
            P(None, "lat", None, None),
            P(),
            P("lat", None, None),
            P("lat"),
            P(),
            P(),
        ),
        out_specs=P("lat", "lon", None),
        check_vma=False,
    )
```

```python
import math

import jax
import jax.numpy as jnp
import numpy as np
from jax import lax
from jax.experimental import pallas as pl
from jax.experimental.pallas import tpu as pltpu
from jax.sharding import PartitionSpec as P

MESH = pl.DeviceIdType.MESH
C = 512
NLON = 1440
MODES = 256
DEGREES = 256
KERNELS = 3
CYCLES = 6
LATS = 64
LONS = 2
DEVS = LATS * LONS
CHIPS = 64
STRIDE = 43
HALF = NLON // LONS
EDGE = 16
WIDE = HALF + 2 * EDGE
TILE = 48
WINDOW = TILE + 2 * EDGE
PAIRS = ((1, 2), (3, 4), (0, 5))
F32, BF16 = jnp.float32, jnp.bfloat16


def dft_constants():
    j = np.arange(NLON, dtype=np.int64)[:, None]
    m = np.arange(MODES, dtype=np.int64)[None, :]
    angle = ((j * m) % NLON).astype(np.float64) * (2.0 * math.pi / NLON)
    pair = np.stack([np.cos(angle), -np.sin(angle)], axis=2) / math.sqrt(NLON)
    table = pair.reshape(LONS, HALF, 2 * MODES).astype(np.float32)
    forward = np.ascontiguousarray(table.transpose(0, 2, 1))
    return jnp.asarray(forward, BF16), jnp.asarray(table, BF16)


def dot(a, b):
    return jnp.dot(a, b, preferred_element_type=F32)


def build_taps(i, taps, band):
    rows = lax.broadcasted_iota(jnp.int32, (TILE, 3 * WINDOW), 0)
    cols = lax.broadcasted_iota(jnp.int32, (TILE, 3 * WINDOW), 1)
    shift = cols - rows
    for k in range(KERNELS):
        total = jnp.zeros((TILE, 3 * WINDOW), F32)
        for a in range(3):
            for b in range(5):
                value = taps[((k * CYCLES + i) * 3 + a) * 5 + b]
                total = jnp.where(shift == a * WINDOW + EDGE - 2 + b, value, total)
        band[k * TILE : (k + 1) * TILE, :] = total.astype(BF16)


def basis_tile(i, t, padded, band, terms):
    start = pl.multiple_of(t * TILE, 16)
    window = padded[pl.ds(i, 3), pl.ds(start, WINDOW), :].reshape(3 * WINDOW, C)
    basis = dot(band[...], window).astype(BF16)
    for k in range(KERNELS):
        terms[pl.ds(start, TILE), k * C : (k + 1) * C] = basis[k * TILE : (k + 1) * TILE]


def basis_inner(i, padded, band, terms):
    @pl.loop(1, HALF // TILE - 1)
    def _(t):
        basis_tile(i, t, padded, band, terms)


def basis_edges(i, padded, band, terms):
    basis_tile(i, 0, padded, band, terms)
    basis_tile(i, HALF // TILE - 1, padded, band, terms)


def mix_terms(i, terms, mix, conv):
    @pl.loop(0, 3)
    def _(t):
        rows = pl.ds(pl.multiple_of(t * 240, 16), 240)
        conv[i, rows, :] = dot(terms[rows, :], mix[...]).astype(BF16)


def dft_pair(p, cycles, quad, forward, conv, spectra, send):
    for s in range(2):

        @pl.loop(0, 2)
        def _(t):
            rows = pl.ds(pl.multiple_of(t * 256, 16), 256)
            spectra[s, rows, :] = dot(forward[rows, :], conv[cycles[s]]) * quad[cycles[s]]

    @pl.loop(0, 8)
    def _(t):
        rows = pl.ds(pl.multiple_of(t * 64, 16), 64)
        first = spectra[0, rows, :].reshape(8, 8, C)
        second = spectra[1, rows, :].reshape(8, 8, C)
        low = lax.broadcasted_iota(jnp.int32, (8, 8, C), 1) < 4
        even = jnp.where(low, first, pltpu.roll(second, 4, 1))
        odd = jnp.where(low, pltpu.roll(first, 4, 1), second)
        both = jnp.stack([even, odd], axis=1).reshape(16, 8, C)
        send[p, pl.ds(t * 16, 16)] = both.astype(BF16)


def spread(p, columns_first):
    shape = (LATS * CYCLES, LATS * 8)
    cycle = lax.broadcasted_iota(jnp.int32, shape, 0)
    col = lax.broadcasted_iota(jnp.int32, shape, 1)
    place = (col // 4) % 2
    within = jnp.where(place == 0, PAIRS[p][0], PAIRS[p][1])
    return jnp.where(cycle == (col // 8) * CYCLES + within, 1.0, 0.0).astype(BF16)


def build_triangle(first_order, legendre, ones, table, turned):
    degree = lax.broadcasted_iota(jnp.int32, (DEGREES, LATS * CYCLES), 0)
    for m in range(2):
        values = legendre[m]
        legendre[m] = jnp.where(degree >= first_order + m, values.astype(F32), 0.0).astype(BF16)
    for p in range(3):
        ones[...] = spread(p, False)
        for m in range(2):
            wide = dot(legendre[m], ones[...])
            col = lax.broadcasted_iota(jnp.int32, wide.shape, 1) % 4
            tall = lax.dot_general(
                ones[...], legendre[m], (((0,), (1,)), ((), ())), preferred_element_type=F32
            )
            row = lax.broadcasted_iota(jnp.int32, tall.shape, 0) % 4
            for c in range(2):
                block = slice((2 * m + c) * DEGREES, (2 * m + c + 1) * DEGREES)
                table[p, block, :] = jnp.where(col == 2 * m + c, wide, 0.0).astype(BF16)
                turned[p, :, block] = jnp.where(row == 2 * m + c, tall, 0.0).astype(BF16)


def legendre_pair(p, received, joined, table, coeffs):
    @pl.loop(0, 8)
    def _(t):
        block = received[p, pl.ds(t * 16, 16)].astype(F32).reshape(8, 2, 8, C)
        total = (block[:, 0] + block[:, 1]).reshape(64, C)
        joined[pl.ds(pl.multiple_of(t * 64, 16), 64), :] = total.astype(BF16)

    @pl.loop(0, 4)
    def _(t):
        rows = pl.ds(pl.multiple_of(t * 256, 16), 256)
        value = dot(table[p, rows, :], joined[...])
        if p == 0:
            coeffs[rows, :] = value
        else:
            coeffs[rows, :] += value


def mix_modes(coeffs, weight, gain, mixed):
    for m in range(2):
        real = coeffs[2 * m * DEGREES : (2 * m + 1) * DEGREES, :].astype(BF16)
        imag = coeffs[(2 * m + 1) * DEGREES : (2 * m + 2) * DEGREES, :].astype(BF16)
        new_real = (dot(real, weight[0]) - dot(imag, weight[1])) * gain[...]
        mixed[2 * m * DEGREES : (2 * m + 1) * DEGREES, :] = new_real.astype(BF16)
        new_imag = (dot(real, weight[1]) + dot(imag, weight[0])) * gain[...]
        mixed[(2 * m + 1) * DEGREES : (2 * m + 2) * DEGREES, :] = new_imag.astype(BF16)


def synth_pair(p, turned, mixed, send):
    @pl.loop(0, 4)
    def _(t):
        rows = pl.ds(pl.multiple_of(t * 128, 16), 128)
        value = dot(turned[p, rows, :], mixed[...]).astype(BF16).reshape(16, 8, C)
        send[p, pl.ds(t * 16, 16)] = value


def inverse_pair(p, cycles, inverse, received, synth, conv, out):
    @pl.loop(0, 8)
    def _(t):
        block = received[p, pl.ds(t * 16, 16)].astype(F32).reshape(8, 2, 8, C)
        first, second = block[:, 0], block[:, 1]
        low = lax.broadcasted_iota(jnp.int32, (8, 8, C), 1) < 4
        rows = pl.ds(pl.multiple_of(t * 64, 16), 64)
        even = jnp.where(low, first, pltpu.roll(second, 4, 1))
        odd = jnp.where(low, pltpu.roll(first, 4, 1), second)
        synth[0, rows, :] = even.reshape(64, C).astype(BF16)
        synth[1, rows, :] = odd.reshape(64, C).astype(BF16)

    for s in range(2):

        @pl.loop(0, 3)
        def _(t):
            rows = pl.ds(pl.multiple_of(t * 240, 16), 240)
            value = dot(inverse[rows, :], synth[s]) + conv[cycles[s], rows, :].astype(F32)
            out[cycles[s], rows, :] = value.astype(BF16)


def halo_copies(field, padded, send_sems, recv_sems):
    lat, lon = lax.axis_index("lat"), lax.axis_index("lon")
    up, down, other = (lat + LATS - 1) % LATS, (lat + 1) % LATS, 1 - lon
    head, body, tail = pl.ds(0, EDGE), pl.ds(EDGE, HALF), pl.ds(EDGE + HALF, EDGE)
    last = pl.ds(HALF - EDGE, EDGE)
    inner = pl.ds(1, CYCLES)
    plan = (
        (field.at[:, last], padded.at[inner, head], (lat, other)),
        (field.at[:, head], padded.at[inner, tail], (lat, other)),
        (field.at[0], padded.at[CYCLES + 1, body], (up, lon)),
        (field.at[CYCLES - 1], padded.at[0, body], (down, lon)),
        (field.at[0, last], padded.at[CYCLES + 1, head], (up, other)),
        (field.at[0, head], padded.at[CYCLES + 1, tail], (up, other)),
        (field.at[CYCLES - 1, last], padded.at[0, head], (down, other)),
        (field.at[CYCLES - 1, head], padded.at[0, tail], (down, other)),
    )
    return [
        pltpu.make_async_remote_copy(
            src_ref=src,
            dst_ref=dst,
            send_sem=send_sems.at[n],
            recv_sem=recv_sems.at[n],
            device_id=target,
            device_id_type=MESH,
        )
        for n, (src, dst, target) in enumerate(plan)
    ]


def partner(s, core):
    lat, lon = lax.axis_index("lat"), lax.axis_index("lon")
    x, z, y = lat // 16, (lat // 4) % 4, (lat // 2) % 2 + 2 * lon
    x, z, y = (x + s // 16) % 4, (z + (s // 4) % 4) % 4, (y + s % 4) % 4
    return ((x * 4 + z) * 2 + y % 2) * 2 + (lat + core) % 2, y // 2


def for_partners(act):
    act(*partner(0, 1))

    def step(s, carry):
        far = (s * STRIDE) % CHIPS
        act(*partner(far, 0))
        act(*partner(far, 1))
        return carry

    lax.fori_loop(1, CHIPS, step, 0)


def scatter(p, pick, received, send_sem, recv_sem):
    me = lax.axis_index("lat") * LONS + lax.axis_index("lon")

    def act(lat, lon):
        pltpu.make_async_remote_copy(
            src_ref=pick(lat, lon),
            dst_ref=received.at[p, me],
            send_sem=send_sem,
            recv_sem=recv_sem,
            device_id=(lat, lon),
            device_id_type=MESH,
        ).start()

    for_partners(act)


def arrival(p, received, send_sem, recv_sem):
    return pltpu.make_async_remote_copy(
        src_ref=received.at[p, pl.ds(0, DEVS - 1)],
        dst_ref=received.at[p, pl.ds(0, DEVS - 1)],
        send_sem=send_sem,
        recv_sem=recv_sem,
        device_id=partner(0, 1),
        device_id_type=MESH,
    )


def kernel(
    taps, quad, field, mix, forward_all, inverse_all, legendre_all, weight, gain, out,
    padded, band, terms, forward, spectra, conv, send, received,
    legendre, ones, table, turned, joined, coeffs, mixed, back, returned, inverse, synth,
    local_sems, halo_send, halo_recv, go_send, go_recv, back_send, back_recv,
):
    lat, lon = lax.axis_index("lat"), lax.axis_index("lon")
    me = lat * LONS + lon
    loads = [
        pltpu.make_async_copy(src, dst, local_sems.at[n])
        for n, (src, dst) in enumerate(
            (
                (field, padded.at[pl.ds(1, CYCLES), pl.ds(EDGE, HALF)]),
                (forward_all.at[lon], forward),
                (inverse_all.at[lon], inverse),
                (legendre_all.at[pl.ds(2 * lon, 2)], legendre),
            )
        )
    ]
    for load in loads:
        load.start()
    barrier = pltpu.get_barrier_semaphore()

    def greet(a, b):
        pl.semaphore_signal(barrier, inc=1, device_id=(a, b), device_id_type=MESH)

    for_partners(greet)
    loads[0].wait()
    build_taps(1, taps, band)
    basis_inner(1, padded, band, terms.at[0])
    pl.semaphore_wait(barrier, DEVS - 1)
    copies = halo_copies(field, padded, halo_send, halo_recv)
    for copy in copies:
        copy.start()
    for load in loads[1:]:
        load.wait()
    for p, cycles in enumerate(PAIRS):
        if p == 2:
            for copy in copies[2:]:
                copy.wait_recv()

            @pl.when(lat == 0)
            def _():
                padded[0] = jnp.zeros((WIDE, C), BF16)

            @pl.when(lat == LATS - 1)
            def _():
                padded[CYCLES + 1] = jnp.zeros((WIDE, C), BF16)

        if p > 0:
            build_taps(cycles[0], taps, band)
            basis_inner(cycles[0], padded, band, terms.at[0])
        else:
            copies[0].wait_recv()
            copies[1].wait_recv()
        basis_edges(cycles[0], padded, band, terms.at[0])
        mix_terms(cycles[0], terms.at[0], mix, conv)
        build_taps(cycles[1], taps, band)
        basis_inner(cycles[1], padded, band, terms.at[1])
        basis_edges(cycles[1], padded, band, terms.at[1])
        mix_terms(cycles[1], terms.at[1], mix, conv)
        dft_pair(p, cycles, quad, forward, conv, spectra, send)
        scatter(
            p, lambda a, b: send.at[p, a * LONS + b], received, go_send.at[p], go_recv.at[p]
        )
        received[p, me] = send[p, me]
    build_triangle(4 * lat + 2 * lon, legendre, ones, table, turned)
    for p in range(3):
        arrival(p, received, go_send.at[p], go_recv.at[p]).wait_recv()
        legendre_pair(p, received, joined, table, coeffs)
    mix_modes(coeffs, weight, gain, mixed)
    for p in range(3):
        synth_pair(p, turned, mixed, back)
        scatter(p, lambda a, b: back.at[p, a], returned, back_send.at[p], back_recv.at[p])
        returned[p, me] = back[p, lat]
    for p, cycles in enumerate(PAIRS):
        arrival(p, returned, back_send.at[p], back_recv.at[p]).wait_recv()
        inverse_pair(p, cycles, inverse, returned, synth, conv, out)
    for copy in copies:
        copy.wait_send()
    for p in range(3):
        arrival(p, received, go_send.at[p], go_recv.at[p]).wait_send()
        arrival(p, returned, back_send.at[p], back_recv.at[p]).wait_send()


VMEM = pl.BlockSpec(memory_space=pltpu.VMEM)
SMEM = pl.BlockSpec(memory_space=pltpu.SMEM)
ANY = pl.BlockSpec(memory_space=pl.ANY)
LIMIT = 60 * 2**20


def body(grid_field, disco_taps, disco_mix, legendre, quad_weights, mix_weight, degree_gain):
    forward_all, inverse_all = dft_constants()
    dma = pltpu.SemaphoreType.DMA
    return pl.pallas_call(
        kernel,
        out_shape=jax.ShapeDtypeStruct((CYCLES, HALF, C), BF16),
        in_specs=[SMEM, SMEM, ANY, VMEM, ANY, ANY, ANY, VMEM, VMEM],
        out_specs=VMEM,
        scratch_shapes=[
            pltpu.VMEM((CYCLES + 2, WIDE, C), BF16),
            pltpu.VMEM((KERNELS * TILE, 3 * WINDOW), BF16),
            pltpu.VMEM((2, HALF, KERNELS * C), BF16),
            pltpu.VMEM((2 * MODES, HALF), BF16),
            pltpu.VMEM((2, 2 * MODES, C), F32),
            pltpu.VMEM((CYCLES, HALF, C), BF16),
            pltpu.VMEM((3, DEVS, 8, C), BF16),
            pltpu.VMEM((3, DEVS, 8, C), BF16),
            pltpu.VMEM((2, DEGREES, LATS * CYCLES), BF16),
            pltpu.VMEM((LATS * CYCLES, LATS * 8), BF16),
            pltpu.VMEM((3, 4 * DEGREES, LATS * 8), BF16),
            pltpu.VMEM((3, LATS * 8, 4 * DEGREES), BF16),
            pltpu.VMEM((LATS * 8, C), BF16),
            pltpu.VMEM((4 * DEGREES, C), F32),
            pltpu.VMEM((4 * DEGREES, C), BF16),
            pltpu.VMEM((3, LATS, 8, C), BF16),
            pltpu.VMEM((3, DEVS, 8, C), BF16),
            pltpu.VMEM((HALF, 2 * MODES), BF16),
            pltpu.VMEM((2, 2 * MODES, C), BF16),
            dma((4,)),
            dma((8,)),
            dma((8,)),
            dma((3,)),
            dma((3,)),
            dma((3,)),
            dma((3,)),
        ],
        compiler_params=pltpu.CompilerParams(
            collective_id=0, has_side_effects=True, vmem_limit_bytes=LIMIT
        ),
    )(
        disco_taps.reshape(-1),
        quad_weights,
        grid_field,
        disco_mix,
        forward_all,
        inverse_all,
        legendre,
        mix_weight,
        degree_gain,
    )


def solution(mesh):
    return jax.shard_map(
        body,
        mesh=mesh,
        in_specs=(
            P("lat", "lon", None),
            P(None, "lat", None, None),
            P(),
            P("lat", None, None),
            P("lat"),
            P(),
            P(),
        ),
        out_specs=P("lat", "lon", None),
        check_vma=False,
    )
```

```python
import math

import jax
import jax.numpy as jnp
import numpy as np
from jax import lax
from jax.experimental import pallas as pl
from jax.experimental.pallas import tpu as pltpu
from jax.sharding import PartitionSpec as P

MESH = pl.DeviceIdType.MESH
C = 512
NLON = 1440
MODES = 256
DEGREES = 256
KERNELS = 3
CYCLES = 6
LATS = 64
LONS = 2
DEVS = LATS * LONS
CHIPS = 64
STRIDE = 43
HALF = NLON // LONS
EDGE = 16
WIDE = HALF + 2 * EDGE
TILE = 48
WINDOW = TILE + 2 * EDGE
PAIRS = ((1, 2), (3, 4), (0, 5))
F32, BF16 = jnp.float32, jnp.bfloat16


def dft_constants():
    j = np.arange(NLON, dtype=np.int64)[:, None]
    m = np.arange(MODES, dtype=np.int64)[None, :]
    angle = ((j * m) % NLON).astype(np.float64) * (2.0 * math.pi / NLON)
    pair = np.stack([np.cos(angle), -np.sin(angle)], axis=2) / math.sqrt(NLON)
    table = pair.reshape(LONS, HALF, 2 * MODES).astype(np.float32)
    forward = np.ascontiguousarray(table.transpose(0, 2, 1))
    return jnp.asarray(forward, BF16), jnp.asarray(table, BF16)


def dot(a, b):
    return jnp.dot(a, b, preferred_element_type=F32)


def build_taps(i, taps, band):
    rows = lax.broadcasted_iota(jnp.int32, (TILE, 3 * WINDOW), 0)
    cols = lax.broadcasted_iota(jnp.int32, (TILE, 3 * WINDOW), 1)
    shift = cols - rows
    for k in range(KERNELS):
        total = jnp.zeros((TILE, 3 * WINDOW), F32)
        for a in range(3):
            for b in range(5):
                value = taps[k, i, a, b]
                total = jnp.where(shift == a * WINDOW + EDGE - 2 + b, value, total)
        band[k * TILE : (k + 1) * TILE, :] = total.astype(BF16)


def basis_tile(i, t, padded, band, terms):
    start = pl.multiple_of(t * TILE, 16)
    window = padded[pl.ds(i, 3), pl.ds(start, WINDOW), :].reshape(3 * WINDOW, C)
    basis = dot(band[...], window).astype(BF16)
    for k in range(KERNELS):
        terms[pl.ds(start, TILE), k * C : (k + 1) * C] = basis[k * TILE : (k + 1) * TILE]


def basis_inner(i, padded, band, terms):
    for t in range(1, HALF // TILE - 1):
        basis_tile(i, t, padded, band, terms)


def basis_edges(i, padded, band, terms):
    for t in (0, HALF // TILE - 1):
        basis_tile(i, t, padded, band, terms)


def mix_terms(i, terms, mix, conv):
    for t in range(3):
        rows = slice(t * 240, (t + 1) * 240)
        conv[i, rows, :] = dot(terms[rows, :], mix[...]).astype(BF16)


def dft_pair(p, cycles, quad, forward, conv, spectra, send):
    for s in range(2):
        spectra[s] = dot(forward[...], conv[cycles[s]]) * quad[cycles[s]]

    @pl.loop(0, 8)
    def _(t):
        rows = pl.ds(pl.multiple_of(t * 64, 16), 64)
        first = spectra[0, rows, :].reshape(8, 8, C)
        second = spectra[1, rows, :].reshape(8, 8, C)
        low = lax.broadcasted_iota(jnp.int32, (8, 8, C), 1) < 4
        even = jnp.where(low, first, pltpu.roll(second, 4, 1))
        odd = jnp.where(low, pltpu.roll(first, 4, 1), second)
        both = jnp.stack([even, odd], axis=1).reshape(16, 8, C)
        send[p, pl.ds(t * 16, 16)] = both.astype(BF16)


def spread(p, columns_first):
    shape = (LATS * CYCLES, LATS * 8)
    cycle = lax.broadcasted_iota(jnp.int32, shape, 0)
    col = lax.broadcasted_iota(jnp.int32, shape, 1)
    place = (col // 4) % 2
    within = jnp.where(place == 0, PAIRS[p][0], PAIRS[p][1])
    return jnp.where(cycle == (col // 8) * CYCLES + within, 1.0, 0.0).astype(BF16)


def build_triangle(first_order, legendre, ones, table, turned):
    degree = lax.broadcasted_iota(jnp.int32, (DEGREES, LATS * CYCLES), 0)
    for m in range(2):
        values = legendre[m]
        legendre[m] = jnp.where(degree >= first_order + m, values.astype(F32), 0.0).astype(BF16)
    for p in range(3):
        ones[...] = spread(p, False)
        for m in range(2):
            wide = dot(legendre[m], ones[...])
            col = lax.broadcasted_iota(jnp.int32, wide.shape, 1) % 4
            tall = lax.dot_general(
                ones[...], legendre[m], (((0,), (1,)), ((), ())), preferred_element_type=F32
            )
            row = lax.broadcasted_iota(jnp.int32, tall.shape, 0) % 4
            for c in range(2):
                block = slice((2 * m + c) * DEGREES, (2 * m + c + 1) * DEGREES)
                table[p, block, :] = jnp.where(col == 2 * m + c, wide, 0.0).astype(BF16)
                turned[p, :, block] = jnp.where(row == 2 * m + c, tall, 0.0).astype(BF16)


def legendre_pair(p, received, joined, table, coeffs):
    @pl.loop(0, 8)
    def _(t):
        block = received[p, pl.ds(t * 16, 16)].astype(F32).reshape(8, 2, 8, C)
        total = (block[:, 0] + block[:, 1]).reshape(64, C)
        joined[pl.ds(pl.multiple_of(t * 64, 16), 64), :] = total.astype(BF16)

    value = dot(table[p], joined[...])
    if p == 0:
        coeffs[...] = value
    else:
        coeffs[...] += value


def mix_modes(coeffs, weight, gain, mixed):
    for m in range(2):
        real = coeffs[2 * m * DEGREES : (2 * m + 1) * DEGREES, :].astype(BF16)
        imag = coeffs[(2 * m + 1) * DEGREES : (2 * m + 2) * DEGREES, :].astype(BF16)
        new_real = (dot(real, weight[0]) - dot(imag, weight[1])) * gain[...]
        mixed[2 * m * DEGREES : (2 * m + 1) * DEGREES, :] = new_real.astype(BF16)
        new_imag = (dot(real, weight[1]) + dot(imag, weight[0])) * gain[...]
        mixed[(2 * m + 1) * DEGREES : (2 * m + 2) * DEGREES, :] = new_imag.astype(BF16)


def synth_pair(p, turned, mixed, send):
    send[p] = dot(turned[p], mixed[...]).astype(BF16).reshape(LATS, 8, C)


def inverse_pair(p, cycles, inverse, received, synth, conv):
    @pl.loop(0, 8)
    def _(t):
        block = received[p, pl.ds(t * 16, 16)].astype(F32).reshape(8, 2, 8, C)
        first, second = block[:, 0], block[:, 1]
        low = lax.broadcasted_iota(jnp.int32, (8, 8, C), 1) < 4
        rows = pl.ds(pl.multiple_of(t * 64, 16), 64)
        even = jnp.where(low, first, pltpu.roll(second, 4, 1))
        odd = jnp.where(low, pltpu.roll(first, 4, 1), second)
        synth[0, rows, :] = even.reshape(64, C).astype(BF16)
        synth[1, rows, :] = odd.reshape(64, C).astype(BF16)

    for s in range(2):
        value = dot(inverse[...], synth[s]) + conv[cycles[s]].astype(F32)
        conv[cycles[s]] = value.astype(BF16)


def halo_copies(field, padded, send_sems, recv_sems):
    lat, lon = lax.axis_index("lat"), lax.axis_index("lon")
    up, down, other = (lat + LATS - 1) % LATS, (lat + 1) % LATS, 1 - lon
    head, body, tail = pl.ds(0, EDGE), pl.ds(EDGE, HALF), pl.ds(EDGE + HALF, EDGE)
    last = pl.ds(HALF - EDGE, EDGE)
    inner = pl.ds(1, CYCLES)
    plan = (
        (field.at[:, last], padded.at[inner, head], (lat, other)),
        (field.at[:, head], padded.at[inner, tail], (lat, other)),
        (field.at[0], padded.at[CYCLES + 1, body], (up, lon)),
        (field.at[CYCLES - 1], padded.at[0, body], (down, lon)),
        (field.at[0, last], padded.at[CYCLES + 1, head], (up, other)),
        (field.at[0, head], padded.at[CYCLES + 1, tail], (up, other)),
        (field.at[CYCLES - 1, last], padded.at[0, head], (down, other)),
        (field.at[CYCLES - 1, head], padded.at[0, tail], (down, other)),
    )
    return [
        pltpu.make_async_remote_copy(
            src_ref=src,
            dst_ref=dst,
            send_sem=send_sems.at[n],
            recv_sem=recv_sems.at[n],
            device_id=target,
            device_id_type=MESH,
        )
        for n, (src, dst, target) in enumerate(plan)
    ]


def partner(s, core):
    lat, lon = lax.axis_index("lat"), lax.axis_index("lon")
    x, z, y = lat >> 4, (lat >> 2) & 3, ((lat >> 1) & 1) + 2 * lon
    x, z, y = (x + (s >> 4)) & 3, (z + (s >> 2)) & 3, (y + s) & 3
    return (x << 4) + (z << 2) + ((y & 1) << 1) + ((lat + core) & 1), y >> 1


def for_partners(act):
    act(*partner(0, 1))

    def step(s, carry):
        far = (s * STRIDE) & (CHIPS - 1)
        act(*partner(far, 0))
        act(*partner(far, 1))
        return carry

    lax.fori_loop(1, CHIPS, step, 0)


def scatter(p, pick, received, send_sem, recv_sem):
    me = lax.axis_index("lat") * LONS + lax.axis_index("lon")

    def act(lat, lon):
        pltpu.make_async_remote_copy(
            src_ref=pick(lat, lon),
            dst_ref=received.at[p, me],
            send_sem=send_sem,
            recv_sem=recv_sem,
            device_id=(lat, lon),
            device_id_type=MESH,
        ).start()

    for_partners(act)


def arrival(p, received, send_sem, recv_sem):
    return pltpu.make_async_remote_copy(
        src_ref=received.at[p, pl.ds(0, DEVS - 1)],
        dst_ref=received.at[p, pl.ds(0, DEVS - 1)],
        send_sem=send_sem,
        recv_sem=recv_sem,
        device_id=partner(0, 1),
        device_id_type=MESH,
    )


def axis_peers():
    far = [16 * d for d in (1, 2, 3)] + [4 * d for d in (1, 2, 3)] + [1, 2, 3]
    return [partner(0, 1)] + [partner(d, 0) for d in far]


def signal_all(semaphore, peers):
    for peer in peers:
        pl.semaphore_signal(semaphore, inc=1, device_id=peer, device_id_type=MESH)


def kernel(
    taps, quad, field, mix_all, forward_all, inverse_all, legendre_all, weight_all, gain_all, out,
    padded, band, terms, mix, forward, spectra, conv, send, received,
    legendre, ones, table, turned, joined, coeffs, weight, gain, mixed,
    back, returned, inverse, synth,
    rounds, local_sems, out_sems, halo_send, halo_recv, go_send, go_recv, back_send, back_recv,
):
    lat, lon = lax.axis_index("lat"), lax.axis_index("lon")
    me = lat * LONS + lon
    up, down, other = (lat + LATS - 1) % LATS, (lat + 1) % LATS, 1 - lon
    barrier = pltpu.get_barrier_semaphore()
    near = axis_peers()
    beside = [(up, lon), (down, lon), (up, other), (down, other)]
    signal_all(barrier, near + beside)
    loads = [
        pltpu.make_async_copy(src, dst, local_sems.at[n])
        for n, (src, dst) in enumerate(
            (
                (field, padded.at[pl.ds(1, CYCLES), pl.ds(EDGE, HALF)]),
                (mix_all, mix),
                (forward_all.at[lon], forward),
                (legendre_all.at[pl.ds(2 * lon, 2)], legendre),
                (weight_all, weight),
                (gain_all, gain),
                (inverse_all.at[lon], inverse),
            )
        )
    ]
    for load in loads:
        load.start()
    pl.semaphore_wait(barrier, len(near) + len(beside))
    copies = halo_copies(field, padded, halo_send, halo_recv)
    for copy in copies:
        copy.start()
    signal_all(rounds.at[0], near)
    loads[0].wait()
    build_taps(1, taps, band)
    basis_inner(1, padded, band, terms.at[0])
    pl.semaphore_wait(rounds.at[0], len(near))
    signal_all(rounds.at[1], near)
    for load in loads[1:]:
        load.wait()
    for p, cycles in enumerate(PAIRS):
        if p == 2:
            for copy in copies[2:]:
                copy.wait_recv()

            @pl.when(lat == 0)
            def _():
                padded[0] = jnp.zeros((WIDE, C), BF16)

            @pl.when(lat == LATS - 1)
            def _():
                padded[CYCLES + 1] = jnp.zeros((WIDE, C), BF16)

        if p > 0:
            build_taps(cycles[0], taps, band)
            basis_inner(cycles[0], padded, band, terms.at[0])
        else:
            copies[0].wait_recv()
            copies[1].wait_recv()
        basis_edges(cycles[0], padded, band, terms.at[0])
        mix_terms(cycles[0], terms.at[0], mix, conv)
        if p == 0:
            pl.semaphore_wait(rounds.at[1], len(near))
            signal_all(rounds.at[2], near)
        build_taps(cycles[1], taps, band)
        basis_inner(cycles[1], padded, band, terms.at[1])
        basis_edges(cycles[1], padded, band, terms.at[1])
        mix_terms(cycles[1], terms.at[1], mix, conv)
        dft_pair(p, cycles, quad, forward, conv, spectra, send)
        if p == 0:
            pl.semaphore_wait(rounds.at[2], len(near))
        scatter(
            p, lambda a, b: send.at[p, a * LONS + b], received, go_send.at[p], go_recv.at[p]
        )
        received[p, me] = send[p, me]
    build_triangle(4 * lat + 2 * lon, legendre, ones, table, turned)
    for p in range(3):
        arrival(p, received, go_send.at[p], go_recv.at[p]).wait_recv()
        legendre_pair(p, received, joined, table, coeffs)
    mix_modes(coeffs, weight, gain, mixed)
    for p in range(3):
        synth_pair(p, turned, mixed, back)
        scatter(p, lambda a, b: back.at[p, a], returned, back_send.at[p], back_recv.at[p])
        returned[p, me] = back[p, lat]
    stores = []
    for p, cycles in enumerate(PAIRS):
        arrival(p, returned, back_send.at[p], back_recv.at[p]).wait_recv()
        inverse_pair(p, cycles, inverse, returned, synth, conv)
        for i in cycles:
            store = pltpu.make_async_copy(conv.at[i], out.at[i], out_sems.at[i])
            store.start()
            stores.append(store)
    for copy in copies:
        copy.wait_send()
    for p in range(3):
        arrival(p, received, go_send.at[p], go_recv.at[p]).wait_send()
        arrival(p, returned, back_send.at[p], back_recv.at[p]).wait_send()
    for store in stores:
        store.wait()


SMEM = pl.BlockSpec(memory_space=pltpu.SMEM)
VMEM = pl.BlockSpec(memory_space=pltpu.VMEM)
ANY = pl.BlockSpec(memory_space=pl.ANY)
LIMIT = 60 * 2**20


def body(grid_field, disco_taps, disco_mix, legendre, quad_weights, mix_weight, degree_gain):
    forward_all, inverse_all = dft_constants()
    dma = pltpu.SemaphoreType.DMA
    return pl.pallas_call(
        kernel,
        out_shape=jax.ShapeDtypeStruct((CYCLES, HALF, C), BF16),
        in_specs=[SMEM, SMEM] + [ANY] * 7,
        out_specs=ANY,
        scratch_shapes=[
            pltpu.VMEM((CYCLES + 2, WIDE, C), BF16),
            pltpu.VMEM((KERNELS * TILE, 3 * WINDOW), BF16),
            pltpu.VMEM((2, HALF, KERNELS * C), BF16),
            pltpu.VMEM((KERNELS * C, C), BF16),
            pltpu.VMEM((2 * MODES, HALF), BF16),
            pltpu.VMEM((2, 2 * MODES, C), F32),
            pltpu.VMEM((CYCLES, HALF, C), BF16),
            pltpu.VMEM((3, DEVS, 8, C), BF16),
            pltpu.VMEM((3, DEVS, 8, C), BF16),
            pltpu.VMEM((2, DEGREES, LATS * CYCLES), BF16),
            pltpu.VMEM((LATS * CYCLES, LATS * 8), BF16),
            pltpu.VMEM((3, 4 * DEGREES, LATS * 8), BF16),
            pltpu.VMEM((3, LATS * 8, 4 * DEGREES), BF16),
            pltpu.VMEM((LATS * 8, C), BF16),
            pltpu.VMEM((4 * DEGREES, C), F32),
            pltpu.VMEM((2, C, C), BF16),
            pltpu.VMEM((DEGREES, C), F32),
            pltpu.VMEM((4 * DEGREES, C), BF16),
            pltpu.VMEM((3, LATS, 8, C), BF16),
            pltpu.VMEM((3, DEVS, 8, C), BF16),
            pltpu.VMEM((HALF, 2 * MODES), BF16),
            pltpu.VMEM((2, 2 * MODES, C), BF16),
            pltpu.SemaphoreType.REGULAR((3,)),
            dma((7,)),
            dma((CYCLES,)),
            dma((8,)),
            dma((8,)),
            dma((3,)),
            dma((3,)),
            dma((3,)),
            dma((3,)),
        ],
        compiler_params=pltpu.CompilerParams(
            collective_id=0, has_side_effects=True, vmem_limit_bytes=LIMIT
        ),
    )(
        disco_taps,
        quad_weights,
        grid_field,
        disco_mix,
        forward_all,
        inverse_all,
        legendre,
        mix_weight,
        degree_gain,
    )


def solution(mesh):
    return jax.shard_map(
        body,
        mesh=mesh,
        in_specs=(
            P("lat", "lon", None),
            P(None, "lat", None, None),
            P(),
            P("lat", None, None),
            P("lat"),
            P(),
            P(),
        ),
        out_specs=P("lat", "lon", None),
        check_vma=False,
    )
```

```python
import math

import jax
import jax.numpy as jnp
import numpy as np
from jax import lax
from jax.experimental import pallas as pl
from jax.experimental.pallas import tpu as pltpu
from jax.sharding import PartitionSpec as P

MESH = pl.DeviceIdType.MESH
C = 512
NLON = 1440
MODES = 256
DEGREES = 256
KERNELS = 3
CYCLES = 6
LATS = 64
LONS = 2
DEVS = LATS * LONS
CHIPS = 64
STRIDE = 43
HALF = NLON // LONS
EDGE = 16
WIDE = HALF + 2 * EDGE
TILE = 48
WINDOW = TILE + 2 * EDGE
PAIRS = ((1, 2), (3, 4), (0, 5))
F32, BF16 = jnp.float32, jnp.bfloat16


def dft_constants():
    j = np.arange(NLON, dtype=np.int64)[:, None]
    m = np.arange(MODES, dtype=np.int64)[None, :]
    angle = ((j * m) % NLON).astype(np.float64) * (2.0 * math.pi / NLON)
    pair = np.stack([np.cos(angle), -np.sin(angle)], axis=2) / math.sqrt(NLON)
    table = pair.reshape(LONS, HALF, 2 * MODES).astype(np.float32)
    forward = np.ascontiguousarray(table.transpose(0, 2, 1))
    return jnp.asarray(forward, BF16), jnp.asarray(table, BF16)


def dot(a, b):
    return jnp.dot(a, b, preferred_element_type=F32)


def build_taps(i, taps, band):
    rows = lax.broadcasted_iota(jnp.int32, (TILE, 3 * WINDOW), 0)
    cols = lax.broadcasted_iota(jnp.int32, (TILE, 3 * WINDOW), 1)
    shift = cols - rows
    for k in range(KERNELS):
        total = jnp.zeros((TILE, 3 * WINDOW), F32)
        for a in range(3):
            for b in range(5):
                value = taps[k, b, a, i]
                total = jnp.where(shift == a * WINDOW + EDGE - 2 + b, value, total)
        band[k * TILE : (k + 1) * TILE, :] = total.astype(BF16)


def basis_tile(i, t, padded, band, terms):
    start = pl.multiple_of(t * TILE, 16)
    window = padded[pl.ds(i, 3), pl.ds(start, WINDOW), :].reshape(3 * WINDOW, C)
    basis = dot(band[...], window).astype(BF16)
    for k in range(KERNELS):
        terms[pl.ds(start, TILE), k * C : (k + 1) * C] = basis[k * TILE : (k + 1) * TILE]


def basis_inner(i, padded, band, terms):
    for t in range(1, HALF // TILE - 1):
        basis_tile(i, t, padded, band, terms)


def basis_edges(i, padded, band, terms):
    for t in (0, HALF // TILE - 1):
        basis_tile(i, t, padded, band, terms)


def mix_terms(i, terms, mix, conv):
    for t in range(3):
        rows = slice(t * 240, (t + 1) * 240)
        conv[i, rows, :] = dot(terms[rows, :], mix[...]).astype(BF16)


def dft_pair(p, cycles, quad, forward, conv, spectra, send):
    for s in range(2):
        spectra[s] = dot(forward[...], conv[cycles[s]]) * quad[cycles[s]]

    @pl.loop(0, 8)
    def _(t):
        rows = pl.ds(pl.multiple_of(t * 64, 16), 64)
        first = spectra[0, rows, :].reshape(8, 8, C)
        second = spectra[1, rows, :].reshape(8, 8, C)
        low = lax.broadcasted_iota(jnp.int32, (8, 8, C), 1) < 4
        even = jnp.where(low, first, pltpu.roll(second, 4, 1))
        odd = jnp.where(low, pltpu.roll(first, 4, 1), second)
        both = jnp.stack([even, odd], axis=1).reshape(16, 8, C)
        send[p, pl.ds(t * 16, 16)] = both.astype(BF16)


def spread(p, columns_first):
    shape = (LATS * CYCLES, LATS * 8)
    cycle = lax.broadcasted_iota(jnp.int32, shape, 0)
    col = lax.broadcasted_iota(jnp.int32, shape, 1)
    place = (col // 4) % 2
    within = jnp.where(place == 0, PAIRS[p][0], PAIRS[p][1])
    return jnp.where(cycle == (col // 8) * CYCLES + within, 1.0, 0.0).astype(BF16)


def build_triangle(first_order, legendre, ones, table, turned):
    degree = lax.broadcasted_iota(jnp.int32, (DEGREES, LATS * CYCLES), 0)
    for m in range(2):
        values = legendre[m]
        legendre[m] = jnp.where(degree >= first_order + m, values.astype(F32), 0.0).astype(BF16)
    for p in range(3):
        ones[...] = spread(p, False)
        for m in range(2):
            wide = dot(legendre[m], ones[...])
            col = lax.broadcasted_iota(jnp.int32, wide.shape, 1) % 4
            tall = lax.dot_general(
                ones[...], legendre[m], (((0,), (1,)), ((), ())), preferred_element_type=F32
            )
            row = lax.broadcasted_iota(jnp.int32, tall.shape, 0) % 4
            for c in range(2):
                block = slice((2 * m + c) * DEGREES, (2 * m + c + 1) * DEGREES)
                table[p, block, :] = jnp.where(col == 2 * m + c, wide, 0.0).astype(BF16)
                turned[p, :, block] = jnp.where(row == 2 * m + c, tall, 0.0).astype(BF16)


def legendre_pair(p, received, joined, table, coeffs):
    @pl.loop(0, 8)
    def _(t):
        block = received[p, pl.ds(t * 16, 16)].astype(F32).reshape(8, 2, 8, C)
        total = (block[:, 0] + block[:, 1]).reshape(64, C)
        joined[pl.ds(pl.multiple_of(t * 64, 16), 64), :] = total.astype(BF16)

    value = dot(table[p], joined[...])
    if p == 0:
        coeffs[...] = value
    else:
        coeffs[...] += value


def mix_modes(coeffs, weight, gain, mixed):
    for m in range(2):
        real = coeffs[2 * m * DEGREES : (2 * m + 1) * DEGREES, :].astype(BF16)
        imag = coeffs[(2 * m + 1) * DEGREES : (2 * m + 2) * DEGREES, :].astype(BF16)
        new_real = (dot(real, weight[0]) - dot(imag, weight[1])) * gain[...]
        mixed[2 * m * DEGREES : (2 * m + 1) * DEGREES, :] = new_real.astype(BF16)
        new_imag = (dot(real, weight[1]) + dot(imag, weight[0])) * gain[...]
        mixed[(2 * m + 1) * DEGREES : (2 * m + 2) * DEGREES, :] = new_imag.astype(BF16)


def synth_pair(p, turned, mixed, send):
    send[p] = dot(turned[p], mixed[...]).astype(BF16).reshape(LATS, 8, C)


def inverse_pair(p, cycles, inverse, received, synth, conv):
    @pl.loop(0, 8)
    def _(t):
        block = received[p, pl.ds(t * 16, 16)].astype(F32).reshape(8, 2, 8, C)
        first, second = block[:, 0], block[:, 1]
        low = lax.broadcasted_iota(jnp.int32, (8, 8, C), 1) < 4
        rows = pl.ds(pl.multiple_of(t * 64, 16), 64)
        even = jnp.where(low, first, pltpu.roll(second, 4, 1))
        odd = jnp.where(low, pltpu.roll(first, 4, 1), second)
        synth[0, rows, :] = even.reshape(64, C).astype(BF16)
        synth[1, rows, :] = odd.reshape(64, C).astype(BF16)

    for s in range(2):
        value = dot(inverse[...], synth[s]) + conv[cycles[s]].astype(F32)
        conv[cycles[s]] = value.astype(BF16)


def halo_copies(field, padded, send_sems, recv_sems):
    lat, lon = lax.axis_index("lat"), lax.axis_index("lon")
    up, down, other = (lat + LATS - 1) % LATS, (lat + 1) % LATS, 1 - lon
    head, body, tail = pl.ds(0, EDGE), pl.ds(EDGE, HALF), pl.ds(EDGE + HALF, EDGE)
    last = pl.ds(HALF - EDGE, EDGE)
    inner = pl.ds(1, CYCLES)
    plan = (
        (field.at[:, last], padded.at[inner, head], (lat, other)),
        (field.at[:, head], padded.at[inner, tail], (lat, other)),
        (field.at[0], padded.at[CYCLES + 1, body], (up, lon)),
        (field.at[CYCLES - 1], padded.at[0, body], (down, lon)),
        (field.at[0, last], padded.at[CYCLES + 1, head], (up, other)),
        (field.at[0, head], padded.at[CYCLES + 1, tail], (up, other)),
        (field.at[CYCLES - 1, last], padded.at[0, head], (down, other)),
        (field.at[CYCLES - 1, head], padded.at[0, tail], (down, other)),
    )
    return [
        pltpu.make_async_remote_copy(
            src_ref=src,
            dst_ref=dst,
            send_sem=send_sems.at[n],
            recv_sem=recv_sems.at[n],
            device_id=target,
            device_id_type=MESH,
        )
        for n, (src, dst, target) in enumerate(plan)
    ]


def partner(s, core):
    lat, lon = lax.axis_index("lat"), lax.axis_index("lon")
    x, z, y = lat >> 4, (lat >> 2) & 3, ((lat >> 1) & 1) + 2 * lon
    x, z, y = (x + (s >> 4)) & 3, (z + (s >> 2)) & 3, (y + s) & 3
    return (x << 4) + (z << 2) + ((y & 1) << 1) + ((lat + core) & 1), y >> 1


def for_partners(act):
    act(*partner(0, 1))

    def step(s, carry):
        far = (s * STRIDE) & (CHIPS - 1)
        act(*partner(far, 0))
        act(*partner(far, 1))
        return carry

    lax.fori_loop(1, CHIPS, step, 0)


def scatter(p, pick, received, send_sem, recv_sem):
    me = lax.axis_index("lat") * LONS + lax.axis_index("lon")

    def act(lat, lon):
        pltpu.make_async_remote_copy(
            src_ref=pick(lat, lon),
            dst_ref=received.at[p, me],
            send_sem=send_sem,
            recv_sem=recv_sem,
            device_id=(lat, lon),
            device_id_type=MESH,
        ).start()

    for_partners(act)


def arrival(p, received, send_sem, recv_sem):
    return pltpu.make_async_remote_copy(
        src_ref=received.at[p, pl.ds(0, DEVS - 1)],
        dst_ref=received.at[p, pl.ds(0, DEVS - 1)],
        send_sem=send_sem,
        recv_sem=recv_sem,
        device_id=partner(0, 1),
        device_id_type=MESH,
    )


def axis_peers():
    far = [16 * d for d in (1, 2, 3)] + [4 * d for d in (1, 2, 3)] + [1, 2, 3]
    return [partner(0, 1)] + [partner(d, 0) for d in far]


def signal_all(semaphore, peers):
    for peer in peers:
        pl.semaphore_signal(semaphore, inc=1, device_id=peer, device_id_type=MESH)


def kernel(
    taps, quad, field, mix_all, forward_all, inverse_all, legendre_all, weight_all, gain_all, conv,
    padded, band, terms, mix, forward, spectra, send, received,
    legendre, ones, table, turned, joined, coeffs, weight, gain, mixed,
    back, returned, inverse, synth,
    rounds, local_sems, halo_send, halo_recv, go_send, go_recv, back_send, back_recv,
):
    lat, lon = lax.axis_index("lat"), lax.axis_index("lon")
    me = lat * LONS + lon
    up, down, other = (lat + LATS - 1) % LATS, (lat + 1) % LATS, 1 - lon
    barrier = pltpu.get_barrier_semaphore()
    near = axis_peers()
    beside = [(up, lon), (down, lon), (up, other), (down, other)]
    signal_all(barrier, near + beside)
    loads = [
        pltpu.make_async_copy(src, dst, local_sems.at[n])
        for n, (src, dst) in enumerate(
            (
                (field, padded.at[pl.ds(1, CYCLES), pl.ds(EDGE, HALF)]),
                (mix_all, mix),
                (forward_all.at[lon], forward),
                (legendre_all.at[pl.ds(2 * lon, 2)], legendre),
                (weight_all, weight),
                (gain_all, gain),
                (inverse_all.at[lon], inverse),
            )
        )
    ]
    for load in loads:
        load.start()
    pl.semaphore_wait(barrier, len(near) + len(beside))
    copies = halo_copies(field, padded, halo_send, halo_recv)
    for copy in copies:
        copy.start()
    signal_all(rounds.at[0], near)
    loads[0].wait()
    build_taps(1, taps, band)
    basis_inner(1, padded, band, terms.at[0])
    pl.semaphore_wait(rounds.at[0], len(near))
    signal_all(rounds.at[1], near)
    for load in loads[1:]:
        load.wait()
    for p, cycles in enumerate(PAIRS):
        if p == 2:
            for copy in copies[2:]:
                copy.wait_recv()

            @pl.when(lat == 0)
            def _():
                padded[0] = jnp.zeros((WIDE, C), BF16)

            @pl.when(lat == LATS - 1)
            def _():
                padded[CYCLES + 1] = jnp.zeros((WIDE, C), BF16)

        if p > 0:
            build_taps(cycles[0], taps, band)
            basis_inner(cycles[0], padded, band, terms.at[0])
        else:
            copies[0].wait_recv()
            copies[1].wait_recv()
        basis_edges(cycles[0], padded, band, terms.at[0])
        mix_terms(cycles[0], terms.at[0], mix, conv)
        if p == 0:
            pl.semaphore_wait(rounds.at[1], len(near))
            signal_all(rounds.at[2], near)
        build_taps(cycles[1], taps, band)
        basis_inner(cycles[1], padded, band, terms.at[1])
        basis_edges(cycles[1], padded, band, terms.at[1])
        mix_terms(cycles[1], terms.at[1], mix, conv)
        dft_pair(p, cycles, quad, forward, conv, spectra, send)
        if p == 0:
            pl.semaphore_wait(rounds.at[2], len(near))
        scatter(
            p, lambda a, b: send.at[p, a * LONS + b], received, go_send.at[p], go_recv.at[p]
        )
        received[p, me] = send[p, me]
    build_triangle(4 * lat + 2 * lon, legendre, ones, table, turned)
    for p in range(3):
        arrival(p, received, go_send.at[p], go_recv.at[p]).wait_recv()
        legendre_pair(p, received, joined, table, coeffs)
    mix_modes(coeffs, weight, gain, mixed)
    for p in range(3):
        synth_pair(p, turned, mixed, back)
        scatter(p, lambda a, b: back.at[p, a], returned, back_send.at[p], back_recv.at[p])
        returned[p, me] = back[p, lat]
    for p, cycles in enumerate(PAIRS):
        arrival(p, returned, back_send.at[p], back_recv.at[p]).wait_recv()
        inverse_pair(p, cycles, inverse, returned, synth, conv)
    for copy in copies:
        copy.wait_send()
    for p in range(3):
        arrival(p, received, go_send.at[p], go_recv.at[p]).wait_send()
        arrival(p, returned, back_send.at[p], back_recv.at[p]).wait_send()


SMEM = pl.BlockSpec(memory_space=pltpu.SMEM)
VMEM = pl.BlockSpec(memory_space=pltpu.VMEM)
ANY = pl.BlockSpec(memory_space=pl.ANY)
LIMIT = 59 * 2**20


def body(grid_field, disco_taps, disco_mix, legendre, quad_weights, mix_weight, degree_gain):
    forward_all, inverse_all = dft_constants()
    dma = pltpu.SemaphoreType.DMA
    return pl.pallas_call(
        kernel,
        out_shape=pltpu.VMEM((CYCLES, HALF, C), BF16),
        in_specs=[SMEM, SMEM] + [ANY] * 7,
        out_specs=VMEM,
        scratch_shapes=[
            pltpu.VMEM((CYCLES + 2, WIDE, C), BF16),
            pltpu.VMEM((KERNELS * TILE, 3 * WINDOW), BF16),
            pltpu.VMEM((2, HALF, KERNELS * C), BF16),
            pltpu.VMEM((KERNELS * C, C), BF16),
            pltpu.VMEM((2 * MODES, HALF), BF16),
            pltpu.VMEM((2, 2 * MODES, C), F32),
            pltpu.VMEM((3, DEVS, 8, C), BF16),
            pltpu.VMEM((3, DEVS, 8, C), BF16),
            pltpu.VMEM((2, DEGREES, LATS * CYCLES), BF16),
            pltpu.VMEM((LATS * CYCLES, LATS * 8), BF16),
            pltpu.VMEM((3, 4 * DEGREES, LATS * 8), BF16),
            pltpu.VMEM((3, LATS * 8, 4 * DEGREES), BF16),
            pltpu.VMEM((LATS * 8, C), BF16),
            pltpu.VMEM((4 * DEGREES, C), F32),
            pltpu.VMEM((2, C, C), BF16),
            pltpu.VMEM((DEGREES, C), F32),
            pltpu.VMEM((4 * DEGREES, C), BF16),
            pltpu.VMEM((3, LATS, 8, C), BF16),
            pltpu.VMEM((3, DEVS, 8, C), BF16),
            pltpu.VMEM((HALF, 2 * MODES), BF16),
            pltpu.VMEM((2, 2 * MODES, C), BF16),
            pltpu.SemaphoreType.REGULAR((3,)),
            dma((7,)),
            dma((8,)),
            dma((8,)),
            dma((3,)),
            dma((3,)),
            dma((3,)),
            dma((3,)),
        ],
        compiler_params=pltpu.CompilerParams(
            collective_id=0, has_side_effects=True, vmem_limit_bytes=LIMIT
        ),
    )(
        disco_taps.transpose(0, 3, 2, 1),
        quad_weights,
        grid_field,
        disco_mix,
        forward_all,
        inverse_all,
        legendre,
        mix_weight,
        degree_gain,
    )


def solution(mesh):
    return jax.shard_map(
        body,
        mesh=mesh,
        in_specs=(
            P("lat", "lon", None),
            P(None, "lat", None, None),
            P(),
            P("lat", None, None),
            P("lat"),
            P(),
            P(),
        ),
        out_specs=P("lat", "lon", None),
        check_vma=False,
    )
```

```python
import math

import jax
import jax.numpy as jnp
import numpy as np
from jax import lax
from jax.experimental import pallas as pl
from jax.experimental.pallas import tpu as pltpu
from jax.sharding import PartitionSpec as P

MESH = pl.DeviceIdType.MESH
C = 512
NLON = 1440
MODES = 256
DEGREES = 256
KERNELS = 3
CYCLES = 6
LATS = 64
LONS = 2
DEVS = LATS * LONS
CHIPS = 64
STRIDE = 43
HALF = NLON // LONS
EDGE = 16
WIDE = HALF + 2 * EDGE
TILE = 48
WINDOW = TILE + 2 * EDGE
INNER = (1, 2, 3, 4)
OUTER = (0, 5)
F32, BF16 = jnp.float32, jnp.bfloat16


def dft_constants():
    j = np.arange(NLON, dtype=np.int64)[:, None]
    m = np.arange(MODES, dtype=np.int64)[None, :]
    angle = ((j * m) % NLON).astype(np.float64) * (2.0 * math.pi / NLON)
    pair = np.stack([np.cos(angle), -np.sin(angle)], axis=2) / math.sqrt(NLON)
    table = pair.reshape(LONS, HALF, 2 * MODES).astype(np.float32)
    forward = np.ascontiguousarray(table.transpose(0, 2, 1))
    return jnp.asarray(forward, BF16), jnp.asarray(table, BF16)


def dot(a, b):
    return jnp.dot(a, b, preferred_element_type=F32)


def build_taps(i, taps, band):
    rows = lax.broadcasted_iota(jnp.int32, (TILE, 3 * WINDOW), 0)
    cols = lax.broadcasted_iota(jnp.int32, (TILE, 3 * WINDOW), 1)
    shift = cols - rows
    for k in range(KERNELS):
        total = jnp.zeros((TILE, 3 * WINDOW), F32)
        for a in range(3):
            for b in range(5):
                value = taps[k, b, a, i]
                total = jnp.where(shift == a * WINDOW + EDGE - 2 + b, value, total)
        band[k * TILE : (k + 1) * TILE, :] = total.astype(BF16)


def basis_tile(i, t, padded, band, terms):
    start = pl.multiple_of(t * TILE, 16)
    window = padded[pl.ds(i, 3), pl.ds(start, WINDOW), :].reshape(3 * WINDOW, C)
    basis = dot(band[...], window).astype(BF16)
    for k in range(KERNELS):
        terms[pl.ds(start, TILE), k * C : (k + 1) * C] = basis[k * TILE : (k + 1) * TILE]


def basis_inner(i, padded, band, terms):
    for t in range(1, HALF // TILE - 1):
        basis_tile(i, t, padded, band, terms)


def basis_edges(i, padded, band, terms):
    for t in (0, HALF // TILE - 1):
        basis_tile(i, t, padded, band, terms)


def mix_terms(i, terms, mix, conv):
    for t in range(3):
        rows = slice(t * 240, (t + 1) * 240)
        conv[i, rows, :] = dot(terms[rows, :], mix[...]).astype(BF16)


def pick_rows(pieces):
    out = None
    for tiles, source, target in pieces:
        turn = (target - source) % 8
        moved = pltpu.roll(tiles, turn, 1) if turn else tiles
        place = lax.broadcasted_iota(jnp.int32, tiles.shape, 1) // 2
        out = moved if out is None else jnp.where(place == target // 2, moved, out)
    return out


def dft_cycle(s, i, quad, forward, conv, spectra):
    spectra[s] = dot(forward[...], conv[i]) * quad[i]


def pack_inner(spectra, send):
    @pl.loop(0, 8)
    def _(t):
        rows = pl.ds(pl.multiple_of(t * 64, 16), 64)
        parts = [spectra[s, rows, :].reshape(8, 8, C) for s in range(4)]
        for m in range(2):
            tiles = [
                pick_rows([(parts[s], 4 * e + 2 * m, 2 * s) for s in range(4)]) for e in range(2)
            ]
            both = jnp.stack(tiles, axis=1).reshape(16, 8, C)
            send[2 * m, pl.ds(t * 16, 16)] = both.astype(BF16)


def pack_outer(spectra, send):
    @pl.loop(0, 8)
    def _(t):
        rows = pl.ds(pl.multiple_of(t * 64, 16), 64)
        parts = [spectra[s, rows, :].reshape(8, 8, C) for s in range(2)]
        tiles = [
            pick_rows([(parts[s], 4 * e + 2 * m, 4 * s + 2 * m) for s in range(2) for m in range(2)])
            for e in range(2)
        ]
        both = jnp.stack(tiles, axis=1).reshape(16, 8, C)
        send[1, pl.ds(t * 16, 16)] = both.astype(BF16)


def spread(g):
    shape = (LATS * CYCLES, LATS * 8)
    cycle = lax.broadcasted_iota(jnp.int32, shape, 0)
    col = lax.broadcasted_iota(jnp.int32, shape, 1)
    row = col % 8
    within = jnp.where(row < 4, OUTER[0], OUTER[1]) if g == 1 else INNER[0] + row // 2
    return jnp.where(cycle == (col // 8) * CYCLES + within, 1.0, 0.0).astype(BF16)


def orders_of(g):
    return {0: (0,), 1: (0, 1), 2: (1,)}[g]


def block_of(g):
    orders = orders_of(g)
    return slice(orders[0] * 2 * DEGREES, (orders[-1] + 1) * 2 * DEGREES)


def build_triangle(first_order, legendre, ones, table, turned):
    degree = lax.broadcasted_iota(jnp.int32, (DEGREES, LATS * CYCLES), 0)
    for m in range(2):
        values = legendre[m]
        legendre[m] = jnp.where(degree >= first_order + m, values.astype(F32), 0.0).astype(BF16)
    for g in range(3):
        if g < 2:
            ones[...] = spread(g)
        else:
            ones[...] = spread(0)
        for m in orders_of(g):
            wide = dot(legendre[m], ones[...])
            tall = lax.dot_general(
                ones[...], legendre[m], (((0,), (1,)), ((), ())), preferred_element_type=F32
            )
            col = lax.broadcasted_iota(jnp.int32, wide.shape, 1)
            row = lax.broadcasted_iota(jnp.int32, tall.shape, 0)
            for c in range(2):
                block = slice((2 * m + c) * DEGREES, (2 * m + c + 1) * DEGREES)
                own, own_row = (
                    (col % 4 == 2 * m + c, row % 4 == 2 * m + c)
                    if g == 1
                    else (col % 2 == c, row % 2 == c)
                )
                table[g, block, :] = jnp.where(own, wide, 0.0).astype(BF16)
                turned[g, :, block] = jnp.where(own_row, tall, 0.0).astype(BF16)


def legendre_group(g, received, joined, table, coeffs):
    @pl.loop(0, 8)
    def _(t):
        block = received[g, pl.ds(t * 16, 16)].astype(F32).reshape(8, 2, 8, C)
        total = (block[:, 0] + block[:, 1]).reshape(64, C)
        joined[pl.ds(pl.multiple_of(t * 64, 16), 64), :] = total.astype(BF16)

    if g == 0:
        coeffs[block_of(0), :] = dot(table[0, block_of(0), :], joined[...])
    elif g == 1:
        coeffs[block_of(0), :] += dot(table[1, block_of(0), :], joined[...])
        coeffs[block_of(2), :] = dot(table[1, block_of(2), :], joined[...])
    else:
        coeffs[block_of(2), :] += dot(table[2, block_of(2), :], joined[...])


def mix_modes(m, coeffs, weight, gain, mixed):
    real = coeffs[2 * m * DEGREES : (2 * m + 1) * DEGREES, :].astype(BF16)
    imag = coeffs[(2 * m + 1) * DEGREES : (2 * m + 2) * DEGREES, :].astype(BF16)
    new_real = (dot(real, weight[0]) - dot(imag, weight[1])) * gain[...]
    mixed[2 * m * DEGREES : (2 * m + 1) * DEGREES, :] = new_real.astype(BF16)
    new_imag = (dot(real, weight[1]) + dot(imag, weight[0])) * gain[...]
    mixed[(2 * m + 1) * DEGREES : (2 * m + 2) * DEGREES, :] = new_imag.astype(BF16)


def synth_group(g, turned, mixed, send):
    value = dot(turned[g, :, block_of(g)], mixed[block_of(g), :])
    send[g] = value.astype(BF16).reshape(LATS, 8, C)


def unpack_inner(received, synth):
    @pl.loop(0, 8)
    def _(t):
        parts = [received[2 * m, pl.ds(t * 16, 16)].astype(F32).reshape(8, 2, 8, C) for m in range(2)]
        rows = pl.ds(pl.multiple_of(t * 64, 16), 64)
        for s in range(4):
            tiles = pick_rows(
                [(parts[m][:, e], 2 * s, 4 * e + 2 * m) for e in range(2) for m in range(2)]
            )
            synth[s, rows, :] = tiles.reshape(64, C).astype(BF16)


def unpack_outer(received, synth):
    @pl.loop(0, 8)
    def _(t):
        part = received[1, pl.ds(t * 16, 16)].astype(F32).reshape(8, 2, 8, C)
        rows = pl.ds(pl.multiple_of(t * 64, 16), 64)
        for s in range(2):
            tiles = pick_rows(
                [(part[:, e], 4 * s + 2 * m, 4 * e + 2 * m) for e in range(2) for m in range(2)]
            )
            synth[s, rows, :] = tiles.reshape(64, C).astype(BF16)


def inverse_cycle(s, i, inverse, synth, conv):
    conv[i] = (dot(inverse[...], synth[s]) + conv[i].astype(F32)).astype(BF16)


def halo_copies(field, padded, send_sems, recv_sems):
    lat, lon = lax.axis_index("lat"), lax.axis_index("lon")
    up, down, other = (lat + LATS - 1) % LATS, (lat + 1) % LATS, 1 - lon
    head, body, tail = pl.ds(0, EDGE), pl.ds(EDGE, HALF), pl.ds(EDGE + HALF, EDGE)
    last = pl.ds(HALF - EDGE, EDGE)
    inner = pl.ds(1, CYCLES)
    plan = (
        (field.at[:, last], padded.at[inner, head], (lat, other)),
        (field.at[:, head], padded.at[inner, tail], (lat, other)),
        (field.at[0], padded.at[CYCLES + 1, body], (up, lon)),
        (field.at[CYCLES - 1], padded.at[0, body], (down, lon)),
        (field.at[0, last], padded.at[CYCLES + 1, head], (up, other)),
        (field.at[0, head], padded.at[CYCLES + 1, tail], (up, other)),
        (field.at[CYCLES - 1, last], padded.at[0, head], (down, other)),
        (field.at[CYCLES - 1, head], padded.at[0, tail], (down, other)),
    )
    return [
        pltpu.make_async_remote_copy(
            src_ref=src,
            dst_ref=dst,
            send_sem=send_sems.at[n],
            recv_sem=recv_sems.at[n],
            device_id=target,
            device_id_type=MESH,
        )
        for n, (src, dst, target) in enumerate(plan)
    ]


def partner(s, core):
    lat, lon = lax.axis_index("lat"), lax.axis_index("lon")
    x, z, y = lat >> 4, (lat >> 2) & 3, ((lat >> 1) & 1) + 2 * lon
    x, z, y = (x + (s >> 4)) & 3, (z + (s >> 2)) & 3, (y + s) & 3
    return (x << 4) + (z << 2) + ((y & 1) << 1) + ((lat + core) & 1), y >> 1


def for_partners(act):
    act(*partner(0, 1))

    def step(s, carry):
        far = (s * STRIDE) & (CHIPS - 1)
        act(*partner(far, 0))
        act(*partner(far, 1))
        return carry

    lax.fori_loop(1, CHIPS, step, 0)


def scatter(p, pick, received, send_sem, recv_sem):
    me = lax.axis_index("lat") * LONS + lax.axis_index("lon")

    def act(lat, lon):
        pltpu.make_async_remote_copy(
            src_ref=pick(lat, lon),
            dst_ref=received.at[p, me],
            send_sem=send_sem,
            recv_sem=recv_sem,
            device_id=(lat, lon),
            device_id_type=MESH,
        ).start()

    for_partners(act)


def arrival(p, received, send_sem, recv_sem):
    return pltpu.make_async_remote_copy(
        src_ref=received.at[p, pl.ds(0, DEVS - 1)],
        dst_ref=received.at[p, pl.ds(0, DEVS - 1)],
        send_sem=send_sem,
        recv_sem=recv_sem,
        device_id=partner(0, 1),
        device_id_type=MESH,
    )


def axis_peers():
    far = [16 * d for d in (1, 2, 3)] + [4 * d for d in (1, 2, 3)] + [1, 2, 3]
    return [partner(0, 1)] + [partner(d, 0) for d in far]


def signal_all(semaphore, peers):
    for peer in peers:
        pl.semaphore_signal(semaphore, inc=1, device_id=peer, device_id_type=MESH)


def kernel(
    taps, quad, field, mix_all, forward_all, inverse_all, legendre_all, weight_all, gain_all, conv,
    padded, band, terms, mix, forward, spectra, send, received,
    legendre, ones, table, turned, joined, coeffs, weight, gain, mixed,
    back, returned, inverse, synth,
    rounds, local_sems, halo_send, halo_recv, go_send, go_recv, back_send, back_recv,
):
    lat, lon = lax.axis_index("lat"), lax.axis_index("lon")
    me = lat * LONS + lon
    up, down, other = (lat + LATS - 1) % LATS, (lat + 1) % LATS, 1 - lon
    barrier = pltpu.get_barrier_semaphore()
    near = axis_peers()
    beside = [(up, lon), (down, lon), (up, other), (down, other)]
    signal_all(barrier, near + beside)
    loads = [
        pltpu.make_async_copy(src, dst, local_sems.at[n])
        for n, (src, dst) in enumerate(
            (
                (field, padded.at[pl.ds(1, CYCLES), pl.ds(EDGE, HALF)]),
                (mix_all, mix),
                (forward_all.at[lon], forward),
                (legendre_all.at[pl.ds(2 * lon, 2)], legendre),
                (weight_all, weight),
                (gain_all, gain),
                (inverse_all.at[lon], inverse),
            )
        )
    ]
    for load in loads:
        load.start()
    pl.semaphore_wait(barrier, len(near) + len(beside))
    copies = halo_copies(field, padded, halo_send, halo_recv)
    for copy in copies:
        copy.start()
    signal_all(rounds.at[0], near)
    loads[0].wait()
    build_taps(1, taps, band)
    basis_inner(1, padded, band, terms.at[0])
    pl.semaphore_wait(rounds.at[0], len(near))
    signal_all(rounds.at[1], near)
    for load in loads[1:]:
        load.wait()
    copies[0].wait_recv()
    copies[1].wait_recv()
    for s, i in enumerate(INNER):
        store = terms.at[s % 2]
        if s > 0:
            build_taps(i, taps, band)
            basis_inner(i, padded, band, store)
        basis_edges(i, padded, band, store)
        mix_terms(i, store, mix, conv)
        if s == 0:
            pl.semaphore_wait(rounds.at[1], len(near))
            signal_all(rounds.at[2], near)
        dft_cycle(s, i, quad, forward, conv, spectra)
    pack_inner(spectra, send)
    pl.semaphore_wait(rounds.at[2], len(near))

    def go(g):
        scatter(
            g, lambda a, b: send.at[g, a * LONS + b], received, go_send.at[g], go_recv.at[g]
        )
        received[g, me] = send[g, me]

    go(0)
    for copy in copies[2:]:
        copy.wait_recv()

    @pl.when(lat == 0)
    def _():
        padded[0] = jnp.zeros((WIDE, C), BF16)

    @pl.when(lat == LATS - 1)
    def _():
        padded[CYCLES + 1] = jnp.zeros((WIDE, C), BF16)

    for s, i in enumerate(OUTER):
        store = terms.at[s]
        build_taps(i, taps, band)
        basis_inner(i, padded, band, store)
        basis_edges(i, padded, band, store)
        mix_terms(i, store, mix, conv)
        dft_cycle(s, i, quad, forward, conv, spectra)
    pack_outer(spectra, send)
    go(1)
    go(2)
    build_triangle(4 * lat + 2 * lon, legendre, ones, table, turned)

    def take(g):
        arrival(g, received, go_send.at[g], go_recv.at[g]).wait_recv()
        legendre_group(g, received, joined, table, coeffs)

    def give(g):
        synth_group(g, turned, mixed, back)
        scatter(g, lambda a, b: back.at[g, a], returned, back_send.at[g], back_recv.at[g])
        returned[g, me] = back[g, lat]

    take(0)
    take(1)
    mix_modes(0, coeffs, weight, gain, mixed)
    give(0)
    take(2)
    mix_modes(1, coeffs, weight, gain, mixed)
    give(2)
    give(1)
    for g in (0, 2):
        arrival(g, returned, back_send.at[g], back_recv.at[g]).wait_recv()
    unpack_inner(returned, synth)
    for s, i in enumerate(INNER):
        inverse_cycle(s, i, inverse, synth, conv)
    arrival(1, returned, back_send.at[1], back_recv.at[1]).wait_recv()
    unpack_outer(returned, synth)
    for s, i in enumerate(OUTER):
        inverse_cycle(s, i, inverse, synth, conv)
    for copy in copies:
        copy.wait_send()
    for p in range(3):
        arrival(p, received, go_send.at[p], go_recv.at[p]).wait_send()
        arrival(p, returned, back_send.at[p], back_recv.at[p]).wait_send()


SMEM = pl.BlockSpec(memory_space=pltpu.SMEM)
VMEM = pl.BlockSpec(memory_space=pltpu.VMEM)
ANY = pl.BlockSpec(memory_space=pl.ANY)
LIMIT = 59 * 2**20


def body(grid_field, disco_taps, disco_mix, legendre, quad_weights, mix_weight, degree_gain):
    forward_all, inverse_all = dft_constants()
    dma = pltpu.SemaphoreType.DMA
    return pl.pallas_call(
        kernel,
        out_shape=pltpu.VMEM((CYCLES, HALF, C), BF16),
        in_specs=[SMEM, SMEM] + [ANY] * 7,
        out_specs=VMEM,
        scratch_shapes=[
            pltpu.VMEM((CYCLES + 2, WIDE, C), BF16),
            pltpu.VMEM((KERNELS * TILE, 3 * WINDOW), BF16),
            pltpu.VMEM((2, HALF, KERNELS * C), BF16),
            pltpu.VMEM((KERNELS * C, C), BF16),
            pltpu.VMEM((2 * MODES, HALF), BF16),
            pltpu.VMEM((4, 2 * MODES, C), F32),
            pltpu.VMEM((3, DEVS, 8, C), BF16),
            pltpu.VMEM((3, DEVS, 8, C), BF16),
            pltpu.VMEM((2, DEGREES, LATS * CYCLES), BF16),
            pltpu.VMEM((LATS * CYCLES, LATS * 8), BF16),
            pltpu.VMEM((3, 4 * DEGREES, LATS * 8), BF16),
            pltpu.VMEM((3, LATS * 8, 4 * DEGREES), BF16),
            pltpu.VMEM((LATS * 8, C), BF16),
            pltpu.VMEM((4 * DEGREES, C), F32),
            pltpu.VMEM((2, C, C), BF16),
            pltpu.VMEM((DEGREES, C), F32),
            pltpu.VMEM((4 * DEGREES, C), BF16),
            pltpu.VMEM((3, LATS, 8, C), BF16),
            pltpu.VMEM((3, DEVS, 8, C), BF16),
            pltpu.VMEM((HALF, 2 * MODES), BF16),
            pltpu.VMEM((4, 2 * MODES, C), BF16),
            pltpu.SemaphoreType.REGULAR((3,)),
            dma((7,)),
            dma((8,)),
            dma((8,)),
            dma((3,)),
            dma((3,)),
            dma((3,)),
            dma((3,)),
        ],
        compiler_params=pltpu.CompilerParams(
            collective_id=0, has_side_effects=True, vmem_limit_bytes=LIMIT
        ),
    )(
        disco_taps.transpose(0, 3, 2, 1),
        quad_weights,
        grid_field,
        disco_mix,
        forward_all,
        inverse_all,
        legendre,
        mix_weight,
        degree_gain,
    )


def solution(mesh):
    return jax.shard_map(
        body,
        mesh=mesh,
        in_specs=(
            P("lat", "lon", None),
            P(None, "lat", None, None),
            P(),
            P("lat", None, None),
            P("lat"),
            P(),
            P(),
        ),
        out_specs=P("lat", "lon", None),
        check_vma=False,
    )
```

```python
import math

import jax
import jax.numpy as jnp
import numpy as np
from jax import lax
from jax.experimental import pallas as pl
from jax.experimental.pallas import tpu as pltpu
from jax.sharding import PartitionSpec as P

MESH = pl.DeviceIdType.MESH
C = 512
NLON = 1440
MODES = 256
DEGREES = 256
KERNELS = 3
CYCLES = 6
LATS = 64
LONS = 2
DEVS = LATS * LONS
CHIPS = 64
STRIDE = 43
HALF = NLON // LONS
EDGE = 16
WIDE = HALF + 2 * EDGE
TILE = 48
WINDOW = TILE + 2 * EDGE
QUAD = (3, 4, 0, 5)
PAIR = (1, 2)
F32, BF16 = jnp.float32, jnp.bfloat16


def dft_constants():
    j = np.arange(NLON, dtype=np.int64)[:, None]
    m = np.arange(MODES, dtype=np.int64)[None, :]
    angle = ((j * m) % NLON).astype(np.float64) * (2.0 * math.pi / NLON)
    pair = np.stack([np.cos(angle), -np.sin(angle)], axis=2) / math.sqrt(NLON)
    table = pair.reshape(LONS, HALF, 2 * MODES).astype(np.float32)
    forward = np.ascontiguousarray(table.transpose(0, 2, 1))
    return jnp.asarray(forward, BF16), jnp.asarray(table, BF16)


def dot(a, b):
    return jnp.dot(a, b, preferred_element_type=F32)


def build_taps(i, taps, band):
    rows = lax.broadcasted_iota(jnp.int32, (TILE, 3 * WINDOW), 0)
    cols = lax.broadcasted_iota(jnp.int32, (TILE, 3 * WINDOW), 1)
    shift = cols - rows
    for k in range(KERNELS):
        total = jnp.zeros((TILE, 3 * WINDOW), F32)
        for a in range(3):
            for b in range(5):
                value = taps[k, b, a, i]
                total = jnp.where(shift == a * WINDOW + EDGE - 2 + b, value, total)
        band[k * TILE : (k + 1) * TILE, :] = total.astype(BF16)


def basis_tile(i, t, padded, band, terms):
    start = pl.multiple_of(t * TILE, 16)
    window = padded[pl.ds(i, 3), pl.ds(start, WINDOW), :].reshape(3 * WINDOW, C)
    basis = dot(band[...], window).astype(BF16)
    for k in range(KERNELS):
        terms[pl.ds(start, TILE), k * C : (k + 1) * C] = basis[k * TILE : (k + 1) * TILE]


def basis_inner(i, padded, band, terms):
    for t in range(1, HALF // TILE - 1):
        basis_tile(i, t, padded, band, terms)


def basis_edges(i, padded, band, terms):
    for t in (0, HALF // TILE - 1):
        basis_tile(i, t, padded, band, terms)


def mix_terms(i, terms, mix, conv):
    for t in range(3):
        rows = slice(t * 240, (t + 1) * 240)
        conv[i, rows, :] = dot(terms[rows, :], mix[...]).astype(BF16)


def pick_rows(pieces):
    out = None
    for tiles, source, target in pieces:
        turn = (target - source) % 8
        moved = pltpu.roll(tiles, turn, 1) if turn else tiles
        place = lax.broadcasted_iota(jnp.int32, tiles.shape, 1) // 2
        out = moved if out is None else jnp.where(place == target // 2, moved, out)
    return out


def dft_cycle(s, i, quad, forward, conv, spectra):
    spectra[s] = dot(forward[...], conv[i]) * quad[i]


def pack_inner(spectra, send):
    @pl.loop(0, 8)
    def _(t):
        rows = pl.ds(pl.multiple_of(t * 64, 16), 64)
        parts = [spectra[s, rows, :].reshape(8, 8, C) for s in range(4)]
        for m in range(2):
            tiles = [
                pick_rows([(parts[s], 4 * e + 2 * m, 2 * s) for s in range(4)]) for e in range(2)
            ]
            both = jnp.stack(tiles, axis=1).reshape(16, 8, C)
            send[2 * m, pl.ds(t * 16, 16)] = both.astype(BF16)


def pack_outer(spectra, send):
    @pl.loop(0, 8)
    def _(t):
        rows = pl.ds(pl.multiple_of(t * 64, 16), 64)
        parts = [spectra[s, rows, :].reshape(8, 8, C) for s in range(2)]
        tiles = [
            pick_rows([(parts[s], 4 * e + 2 * m, 4 * s + 2 * m) for s in range(2) for m in range(2)])
            for e in range(2)
        ]
        both = jnp.stack(tiles, axis=1).reshape(16, 8, C)
        send[1, pl.ds(t * 16, 16)] = both.astype(BF16)


def spread(g):
    shape = (LATS * CYCLES, LATS * 8)
    cycle = lax.broadcasted_iota(jnp.int32, shape, 0)
    col = lax.broadcasted_iota(jnp.int32, shape, 1)
    row = col % 8
    if g == 1:
        within = jnp.where(row < 4, PAIR[0], PAIR[1])
    else:
        late = jnp.where(row < 6, QUAD[2], QUAD[3])
        within = jnp.where(row < 2, QUAD[0], jnp.where(row < 4, QUAD[1], late))
    return jnp.where(cycle == (col // 8) * CYCLES + within, 1.0, 0.0).astype(BF16)


def orders_of(g):
    return {0: (0,), 1: (0, 1), 2: (1,)}[g]


def block_of(g):
    orders = orders_of(g)
    return slice(orders[0] * 2 * DEGREES, (orders[-1] + 1) * 2 * DEGREES)


def build_triangle(first_order, legendre, ones, table, turned):
    degree = lax.broadcasted_iota(jnp.int32, (DEGREES, LATS * CYCLES), 0)
    for m in range(2):
        values = legendre[m]
        legendre[m] = jnp.where(degree >= first_order + m, values.astype(F32), 0.0).astype(BF16)
    for g in range(3):
        if g < 2:
            ones[...] = spread(g)
        else:
            ones[...] = spread(0)
        for m in orders_of(g):
            wide = dot(legendre[m], ones[...])
            tall = lax.dot_general(
                ones[...], legendre[m], (((0,), (1,)), ((), ())), preferred_element_type=F32
            )
            col = lax.broadcasted_iota(jnp.int32, wide.shape, 1)
            row = lax.broadcasted_iota(jnp.int32, tall.shape, 0)
            for c in range(2):
                block = slice((2 * m + c) * DEGREES, (2 * m + c + 1) * DEGREES)
                own, own_row = (
                    (col % 4 == 2 * m + c, row % 4 == 2 * m + c)
                    if g == 1
                    else (col % 2 == c, row % 2 == c)
                )
                table[g, block, :] = jnp.where(own, wide, 0.0).astype(BF16)
                turned[g, :, block] = jnp.where(own_row, tall, 0.0).astype(BF16)


def legendre_group(g, received, joined, table, coeffs):
    @pl.loop(0, 8)
    def _(t):
        block = received[g, pl.ds(t * 16, 16)].astype(F32).reshape(8, 2, 8, C)
        total = (block[:, 0] + block[:, 1]).reshape(64, C)
        joined[pl.ds(pl.multiple_of(t * 64, 16), 64), :] = total.astype(BF16)

    value = dot(table[g, block_of(g), :], joined[...])
    if g == 1:
        coeffs[...] = value
    else:
        coeffs[block_of(g), :] += value


def mix_modes(m, coeffs, weight, gain, mixed):
    real = coeffs[2 * m * DEGREES : (2 * m + 1) * DEGREES, :].astype(BF16)
    imag = coeffs[(2 * m + 1) * DEGREES : (2 * m + 2) * DEGREES, :].astype(BF16)
    new_real = (dot(real, weight[0]) - dot(imag, weight[1])) * gain[...]
    mixed[2 * m * DEGREES : (2 * m + 1) * DEGREES, :] = new_real.astype(BF16)
    new_imag = (dot(real, weight[1]) + dot(imag, weight[0])) * gain[...]
    mixed[(2 * m + 1) * DEGREES : (2 * m + 2) * DEGREES, :] = new_imag.astype(BF16)


def synth_group(g, turned, mixed, send):
    value = dot(turned[g, :, block_of(g)], mixed[block_of(g), :])
    send[g] = value.astype(BF16).reshape(LATS, 8, C)


def unpack_inner(received, synth):
    @pl.loop(0, 8)
    def _(t):
        parts = [received[2 * m, pl.ds(t * 16, 16)].astype(F32).reshape(8, 2, 8, C) for m in range(2)]
        rows = pl.ds(pl.multiple_of(t * 64, 16), 64)
        for s in range(4):
            tiles = pick_rows(
                [(parts[m][:, e], 2 * s, 4 * e + 2 * m) for e in range(2) for m in range(2)]
            )
            synth[s, rows, :] = tiles.reshape(64, C).astype(BF16)


def unpack_outer(received, synth):
    @pl.loop(0, 8)
    def _(t):
        part = received[1, pl.ds(t * 16, 16)].astype(F32).reshape(8, 2, 8, C)
        rows = pl.ds(pl.multiple_of(t * 64, 16), 64)
        for s in range(2):
            tiles = pick_rows(
                [(part[:, e], 4 * s + 2 * m, 4 * e + 2 * m) for e in range(2) for m in range(2)]
            )
            synth[s, rows, :] = tiles.reshape(64, C).astype(BF16)


def inverse_cycle(s, i, inverse, synth, conv):
    conv[i] = (dot(inverse[...], synth[s]) + conv[i].astype(F32)).astype(BF16)


def halo_copies(field, padded, send_sems, recv_sems):
    lat, lon = lax.axis_index("lat"), lax.axis_index("lon")
    up, down, other = (lat + LATS - 1) % LATS, (lat + 1) % LATS, 1 - lon
    head, body, tail = pl.ds(0, EDGE), pl.ds(EDGE, HALF), pl.ds(EDGE + HALF, EDGE)
    last = pl.ds(HALF - EDGE, EDGE)
    inner = pl.ds(1, CYCLES)
    plan = (
        (field.at[:, last], padded.at[inner, head], (lat, other)),
        (field.at[:, head], padded.at[inner, tail], (lat, other)),
        (field.at[0], padded.at[CYCLES + 1, body], (up, lon)),
        (field.at[CYCLES - 1], padded.at[0, body], (down, lon)),
        (field.at[0, last], padded.at[CYCLES + 1, head], (up, other)),
        (field.at[0, head], padded.at[CYCLES + 1, tail], (up, other)),
        (field.at[CYCLES - 1, last], padded.at[0, head], (down, other)),
        (field.at[CYCLES - 1, head], padded.at[0, tail], (down, other)),
    )
    return [
        pltpu.make_async_remote_copy(
            src_ref=src,
            dst_ref=dst,
            send_sem=send_sems.at[n],
            recv_sem=recv_sems.at[n],
            device_id=target,
            device_id_type=MESH,
        )
        for n, (src, dst, target) in enumerate(plan)
    ]


def partner(s, core):
    lat, lon = lax.axis_index("lat"), lax.axis_index("lon")
    x, z, y = lat >> 4, (lat >> 2) & 3, ((lat >> 1) & 1) + 2 * lon
    x, z, y = (x + (s >> 4)) & 3, (z + (s >> 2)) & 3, (y + s) & 3
    return (x << 4) + (z << 2) + ((y & 1) << 1) + ((lat + core) & 1), y >> 1


def for_partners(act):
    act(*partner(0, 1))

    def step(s, carry):
        far = (s * STRIDE) & (CHIPS - 1)
        act(*partner(far, 0))
        act(*partner(far, 1))
        return carry

    lax.fori_loop(1, CHIPS, step, 0)


def scatter(p, pick, received, send_sem, recv_sem):
    me = lax.axis_index("lat") * LONS + lax.axis_index("lon")

    def act(lat, lon):
        pltpu.make_async_remote_copy(
            src_ref=pick(lat, lon),
            dst_ref=received.at[p, me],
            send_sem=send_sem,
            recv_sem=recv_sem,
            device_id=(lat, lon),
            device_id_type=MESH,
        ).start()

    for_partners(act)


def arrival(p, received, send_sem, recv_sem):
    return pltpu.make_async_remote_copy(
        src_ref=received.at[p, pl.ds(0, DEVS - 1)],
        dst_ref=received.at[p, pl.ds(0, DEVS - 1)],
        send_sem=send_sem,
        recv_sem=recv_sem,
        device_id=partner(0, 1),
        device_id_type=MESH,
    )


def axis_peers():
    far = [16 * d for d in (1, 2, 3)] + [4 * d for d in (1, 2, 3)] + [1, 2, 3]
    return [partner(0, 1)] + [partner(d, 0) for d in far]


def signal_all(semaphore, peers):
    for peer in peers:
        pl.semaphore_signal(semaphore, inc=1, device_id=peer, device_id_type=MESH)


def kernel(
    taps, quad, field, mix_all, forward_all, inverse_all, legendre_all, weight_all, gain_all, conv,
    padded, band, terms, mix, forward, spectra, send, received,
    legendre, ones, table, turned, joined, coeffs, weight, gain, mixed,
    back, returned, inverse, synth,
    rounds, local_sems, halo_send, halo_recv, go_send, go_recv, back_send, back_recv,
):
    lat, lon = lax.axis_index("lat"), lax.axis_index("lon")
    me = lat * LONS + lon
    up, down, other = (lat + LATS - 1) % LATS, (lat + 1) % LATS, 1 - lon
    barrier = pltpu.get_barrier_semaphore()
    near = axis_peers()
    beside = [(up, lon), (down, lon), (up, other), (down, other)]
    signal_all(barrier, near + beside)
    loads = [
        pltpu.make_async_copy(src, dst, local_sems.at[n])
        for n, (src, dst) in enumerate(
            (
                (field, padded.at[pl.ds(1, CYCLES), pl.ds(EDGE, HALF)]),
                (mix_all, mix),
                (forward_all.at[lon], forward),
                (legendre_all.at[pl.ds(2 * lon, 2)], legendre),
                (weight_all, weight),
                (gain_all, gain),
                (inverse_all.at[lon], inverse),
            )
        )
    ]
    for load in loads:
        load.start()
    pl.semaphore_wait(barrier, len(near) + len(beside))
    copies = halo_copies(field, padded, halo_send, halo_recv)
    for copy in copies:
        copy.start()
    signal_all(rounds.at[0], near)
    loads[0].wait()
    build_taps(1, taps, band)
    basis_inner(1, padded, band, terms.at[0])
    pl.semaphore_wait(rounds.at[0], len(near))
    signal_all(rounds.at[1], near)
    for load in loads[1:]:
        load.wait()
    copies[0].wait_recv()
    copies[1].wait_recv()

    def go(g):
        scatter(
            g, lambda a, b: send.at[g, a * LONS + b], received, go_send.at[g], go_recv.at[g]
        )
        received[g, me] = send[g, me]

    def convolve(s, i, ready):
        store = terms.at[s % 2]
        if not ready:
            build_taps(i, taps, band)
            basis_inner(i, padded, band, store)
        basis_edges(i, padded, band, store)
        mix_terms(i, store, mix, conv)
        dft_cycle(s, i, quad, forward, conv, spectra)

    convolve(0, PAIR[0], True)
    pl.semaphore_wait(rounds.at[1], len(near))
    signal_all(rounds.at[2], near)
    convolve(1, PAIR[1], False)
    pack_outer(spectra, send)
    pl.semaphore_wait(rounds.at[2], len(near))
    go(1)
    convolve(0, QUAD[0], False)
    convolve(1, QUAD[1], False)
    for copy in copies[2:]:
        copy.wait_recv()

    @pl.when(lat == 0)
    def _():
        padded[0] = jnp.zeros((WIDE, C), BF16)

    @pl.when(lat == LATS - 1)
    def _():
        padded[CYCLES + 1] = jnp.zeros((WIDE, C), BF16)

    convolve(2, QUAD[2], False)
    convolve(3, QUAD[3], False)
    pack_inner(spectra, send)
    go(0)
    go(2)
    build_triangle(4 * lat + 2 * lon, legendre, ones, table, turned)

    def take(g):
        arrival(g, received, go_send.at[g], go_recv.at[g]).wait_recv()
        legendre_group(g, received, joined, table, coeffs)

    def give(g):
        synth_group(g, turned, mixed, back)
        scatter(g, lambda a, b: back.at[g, a], returned, back_send.at[g], back_recv.at[g])
        returned[g, me] = back[g, lat]

    take(1)
    take(0)
    mix_modes(0, coeffs, weight, gain, mixed)
    give(0)
    take(2)
    mix_modes(1, coeffs, weight, gain, mixed)
    give(2)
    give(1)
    for g in (0, 2):
        arrival(g, returned, back_send.at[g], back_recv.at[g]).wait_recv()
    unpack_inner(returned, synth)
    for s, i in enumerate(QUAD):
        inverse_cycle(s, i, inverse, synth, conv)
    arrival(1, returned, back_send.at[1], back_recv.at[1]).wait_recv()
    unpack_outer(returned, synth)
    for s, i in enumerate(PAIR):
        inverse_cycle(s, i, inverse, synth, conv)
    for copy in copies:
        copy.wait_send()
    for p in range(3):
        arrival(p, received, go_send.at[p], go_recv.at[p]).wait_send()
        arrival(p, returned, back_send.at[p], back_recv.at[p]).wait_send()


SMEM = pl.BlockSpec(memory_space=pltpu.SMEM)
VMEM = pl.BlockSpec(memory_space=pltpu.VMEM)
ANY = pl.BlockSpec(memory_space=pl.ANY)
LIMIT = 59 * 2**20


def body(grid_field, disco_taps, disco_mix, legendre, quad_weights, mix_weight, degree_gain):
    forward_all, inverse_all = dft_constants()
    dma = pltpu.SemaphoreType.DMA
    return pl.pallas_call(
        kernel,
        out_shape=pltpu.VMEM((CYCLES, HALF, C), BF16),
        in_specs=[SMEM, SMEM] + [ANY] * 7,
        out_specs=VMEM,
        scratch_shapes=[
            pltpu.VMEM((CYCLES + 2, WIDE, C), BF16),
            pltpu.VMEM((KERNELS * TILE, 3 * WINDOW), BF16),
            pltpu.VMEM((2, HALF, KERNELS * C), BF16),
            pltpu.VMEM((KERNELS * C, C), BF16),
            pltpu.VMEM((2 * MODES, HALF), BF16),
            pltpu.VMEM((4, 2 * MODES, C), F32),
            pltpu.VMEM((3, DEVS, 8, C), BF16),
            pltpu.VMEM((3, DEVS, 8, C), BF16),
            pltpu.VMEM((2, DEGREES, LATS * CYCLES), BF16),
            pltpu.VMEM((LATS * CYCLES, LATS * 8), BF16),
            pltpu.VMEM((3, 4 * DEGREES, LATS * 8), BF16),
            pltpu.VMEM((3, LATS * 8, 4 * DEGREES), BF16),
            pltpu.VMEM((LATS * 8, C), BF16),
            pltpu.VMEM((4 * DEGREES, C), F32),
            pltpu.VMEM((2, C, C), BF16),
            pltpu.VMEM((DEGREES, C), F32),
            pltpu.VMEM((4 * DEGREES, C), BF16),
            pltpu.VMEM((3, LATS, 8, C), BF16),
            pltpu.VMEM((3, DEVS, 8, C), BF16),
            pltpu.VMEM((HALF, 2 * MODES), BF16),
            pltpu.VMEM((4, 2 * MODES, C), BF16),
            pltpu.SemaphoreType.REGULAR((3,)),
            dma((7,)),
            dma((8,)),
            dma((8,)),
            dma((3,)),
            dma((3,)),
            dma((3,)),
            dma((3,)),
        ],
        compiler_params=pltpu.CompilerParams(
            collective_id=0, has_side_effects=True, vmem_limit_bytes=LIMIT
        ),
    )(
        disco_taps.transpose(0, 3, 2, 1),
        quad_weights,
        grid_field,
        disco_mix,
        forward_all,
        inverse_all,
        legendre,
        mix_weight,
        degree_gain,
    )


def solution(mesh):
    return jax.shard_map(
        body,
        mesh=mesh,
        in_specs=(
            P("lat", "lon", None),
            P(None, "lat", None, None),
            P(),
            P("lat", None, None),
            P("lat"),
            P(),
            P(),
        ),
        out_specs=P("lat", "lon", None),
        check_vma=False,
    )
```

```python
import math

import jax
import jax.numpy as jnp
import numpy as np
from jax import lax
from jax.experimental import pallas as pl
from jax.experimental.pallas import tpu as pltpu
from jax.sharding import PartitionSpec as P

MESH = pl.DeviceIdType.MESH
C = 512
NLON = 1440
MODES = 256
DEGREES = 256
KERNELS = 3
CYCLES = 6
LATS = 64
LONS = 2
DEVS = LATS * LONS
CHIPS = 64
STRIDE = 27
HALF = NLON // LONS
EDGE = 16
WIDE = HALF + 2 * EDGE
TILE = 48
WINDOW = TILE + 2 * EDGE
INNER = (1, 2, 3, 4)
OUTER = (0, 5)
F32, BF16 = jnp.float32, jnp.bfloat16


def dft_constants():
    j = np.arange(NLON, dtype=np.int64)[:, None]
    m = np.arange(MODES, dtype=np.int64)[None, :]
    angle = ((j * m) % NLON).astype(np.float64) * (2.0 * math.pi / NLON)
    pair = np.stack([np.cos(angle), -np.sin(angle)], axis=2) / math.sqrt(NLON)
    table = pair.reshape(LONS, HALF, 2 * MODES).astype(np.float32)
    forward = np.ascontiguousarray(table.transpose(0, 2, 1))
    return jnp.asarray(forward, BF16), jnp.asarray(table, BF16)


def dot(a, b):
    return jnp.dot(a, b, preferred_element_type=F32)


def build_taps(i, taps, band):
    rows = lax.broadcasted_iota(jnp.int32, (TILE, 3 * WINDOW), 0)
    cols = lax.broadcasted_iota(jnp.int32, (TILE, 3 * WINDOW), 1)
    shift = cols - rows
    for k in range(KERNELS):
        total = jnp.zeros((TILE, 3 * WINDOW), F32)
        for a in range(3):
            for b in range(5):
                value = taps[k, b, a, i]
                total = jnp.where(shift == a * WINDOW + EDGE - 2 + b, value, total)
        band[k * TILE : (k + 1) * TILE, :] = total.astype(BF16)


def basis_tile(i, t, padded, band, terms):
    start = pl.multiple_of(t * TILE, 16)
    window = padded[pl.ds(i, 3), pl.ds(start, WINDOW), :].reshape(3 * WINDOW, C)
    basis = dot(band[...], window).astype(BF16)
    for k in range(KERNELS):
        terms[pl.ds(start, TILE), k * C : (k + 1) * C] = basis[k * TILE : (k + 1) * TILE]


def basis_inner(i, padded, band, terms):
    for t in range(1, HALF // TILE - 1):
        basis_tile(i, t, padded, band, terms)


def basis_edges(i, padded, band, terms):
    for t in (0, HALF // TILE - 1):
        basis_tile(i, t, padded, band, terms)


def mix_terms(i, terms, mix, conv):
    for t in range(3):
        rows = slice(t * 240, (t + 1) * 240)
        conv[i, rows, :] = dot(terms[rows, :], mix[...]).astype(BF16)


def pick_rows(pieces):
    out = None
    for tiles, source, target in pieces:
        turn = (target - source) % 8
        moved = pltpu.roll(tiles, turn, 1) if turn else tiles
        place = lax.broadcasted_iota(jnp.int32, tiles.shape, 1) // 2
        out = moved if out is None else jnp.where(place == target // 2, moved, out)
    return out


def dft_cycle(s, i, quad, forward, conv, spectra):
    spectra[s] = dot(forward[...], conv[i]) * quad[i]


def pack_inner(spectra, send):
    @pl.loop(0, 8)
    def _(t):
        rows = pl.ds(pl.multiple_of(t * 64, 16), 64)
        parts = [spectra[s, rows, :].reshape(8, 8, C) for s in range(4)]
        for m in range(2):
            tiles = [
                pick_rows([(parts[s], 4 * e + 2 * m, 2 * s) for s in range(4)]) for e in range(2)
            ]
            both = jnp.stack(tiles, axis=1).reshape(16, 8, C)
            send[2 * m, pl.ds(t * 16, 16)] = both.astype(BF16)


def pack_outer(spectra, send):
    @pl.loop(0, 8)
    def _(t):
        rows = pl.ds(pl.multiple_of(t * 64, 16), 64)
        parts = [spectra[s, rows, :].reshape(8, 8, C) for s in range(2)]
        tiles = [
            pick_rows([(parts[s], 4 * e + 2 * m, 4 * s + 2 * m) for s in range(2) for m in range(2)])
            for e in range(2)
        ]
        both = jnp.stack(tiles, axis=1).reshape(16, 8, C)
        send[1, pl.ds(t * 16, 16)] = both.astype(BF16)


def spread(g):
    shape = (LATS * CYCLES, LATS * 8)
    cycle = lax.broadcasted_iota(jnp.int32, shape, 0)
    col = lax.broadcasted_iota(jnp.int32, shape, 1)
    row = col % 8
    within = jnp.where(row < 4, OUTER[0], OUTER[1]) if g == 1 else INNER[0] + row // 2
    return jnp.where(cycle == (col // 8) * CYCLES + within, 1.0, 0.0).astype(BF16)


def orders_of(g):
    return {0: (0,), 1: (0, 1), 2: (1,)}[g]


def block_of(g):
    orders = orders_of(g)
    return slice(orders[0] * 2 * DEGREES, (orders[-1] + 1) * 2 * DEGREES)


def build_triangle(first_order, legendre, ones, table, turned):
    degree = lax.broadcasted_iota(jnp.int32, (DEGREES, LATS * CYCLES), 0)
    for m in range(2):
        values = legendre[m]
        legendre[m] = jnp.where(degree >= first_order + m, values.astype(F32), 0.0).astype(BF16)
    for g in range(3):
        if g < 2:
            ones[...] = spread(g)
        else:
            ones[...] = spread(0)
        for m in orders_of(g):
            wide = dot(legendre[m], ones[...])
            tall = lax.dot_general(
                ones[...], legendre[m], (((0,), (1,)), ((), ())), preferred_element_type=F32
            )
            col = lax.broadcasted_iota(jnp.int32, wide.shape, 1)
            row = lax.broadcasted_iota(jnp.int32, tall.shape, 0)
            for c in range(2):
                block = slice((2 * m + c) * DEGREES, (2 * m + c + 1) * DEGREES)
                own, own_row = (
                    (col % 4 == 2 * m + c, row % 4 == 2 * m + c)
                    if g == 1
                    else (col % 2 == c, row % 2 == c)
                )
                table[g, block, :] = jnp.where(own, wide, 0.0).astype(BF16)
                turned[g, :, block] = jnp.where(own_row, tall, 0.0).astype(BF16)


def legendre_group(g, received, joined, table, coeffs):
    @pl.loop(0, 8)
    def _(t):
        block = received[g, pl.ds(t * 16, 16)].astype(F32).reshape(8, 2, 8, C)
        total = (block[:, 0] + block[:, 1]).reshape(64, C)
        joined[pl.ds(pl.multiple_of(t * 64, 16), 64), :] = total.astype(BF16)

    if g == 0:
        coeffs[block_of(0), :] = dot(table[0, block_of(0), :], joined[...])
    elif g == 1:
        coeffs[block_of(0), :] += dot(table[1, block_of(0), :], joined[...])
        coeffs[block_of(2), :] = dot(table[1, block_of(2), :], joined[...])
    else:
        coeffs[block_of(2), :] += dot(table[2, block_of(2), :], joined[...])


def mix_modes(m, coeffs, weight, gain, mixed):
    real = coeffs[2 * m * DEGREES : (2 * m + 1) * DEGREES, :].astype(BF16)
    imag = coeffs[(2 * m + 1) * DEGREES : (2 * m + 2) * DEGREES, :].astype(BF16)
    new_real = (dot(real, weight[0]) - dot(imag, weight[1])) * gain[...]
    mixed[2 * m * DEGREES : (2 * m + 1) * DEGREES, :] = new_real.astype(BF16)
    new_imag = (dot(real, weight[1]) + dot(imag, weight[0])) * gain[...]
    mixed[(2 * m + 1) * DEGREES : (2 * m + 2) * DEGREES, :] = new_imag.astype(BF16)


def synth_group(g, turned, mixed, send):
    value = dot(turned[g, :, block_of(g)], mixed[block_of(g), :])
    send[g] = value.astype(BF16).reshape(LATS, 8, C)


def unpack_inner(received, synth):
    @pl.loop(0, 8)
    def _(t):
        parts = [received[2 * m, pl.ds(t * 16, 16)].astype(F32).reshape(8, 2, 8, C) for m in range(2)]
        rows = pl.ds(pl.multiple_of(t * 64, 16), 64)
        for s in range(4):
            tiles = pick_rows(
                [(parts[m][:, e], 2 * s, 4 * e + 2 * m) for e in range(2) for m in range(2)]
            )
            synth[s, rows, :] = tiles.reshape(64, C).astype(BF16)


def unpack_outer(received, synth):
    @pl.loop(0, 8)
    def _(t):
        part = received[1, pl.ds(t * 16, 16)].astype(F32).reshape(8, 2, 8, C)
        rows = pl.ds(pl.multiple_of(t * 64, 16), 64)
        for s in range(2):
            tiles = pick_rows(
                [(part[:, e], 4 * s + 2 * m, 4 * e + 2 * m) for e in range(2) for m in range(2)]
            )
            synth[s, rows, :] = tiles.reshape(64, C).astype(BF16)


def inverse_cycle(s, i, inverse, synth, conv):
    conv[i] = (dot(inverse[...], synth[s]) + conv[i].astype(F32)).astype(BF16)


def halo_copies(field, padded, send_sems, recv_sems):
    lat, lon = lax.axis_index("lat"), lax.axis_index("lon")
    up, down, other = (lat + LATS - 1) % LATS, (lat + 1) % LATS, 1 - lon
    head, body, tail = pl.ds(0, EDGE), pl.ds(EDGE, HALF), pl.ds(EDGE + HALF, EDGE)
    last = pl.ds(HALF - EDGE, EDGE)
    inner = pl.ds(1, CYCLES)
    plan = (
        (field.at[:, last], padded.at[inner, head], (lat, other)),
        (field.at[:, head], padded.at[inner, tail], (lat, other)),
        (field.at[0], padded.at[CYCLES + 1, body], (up, lon)),
        (field.at[CYCLES - 1], padded.at[0, body], (down, lon)),
        (field.at[0, last], padded.at[CYCLES + 1, head], (up, other)),
        (field.at[0, head], padded.at[CYCLES + 1, tail], (up, other)),
        (field.at[CYCLES - 1, last], padded.at[0, head], (down, other)),
        (field.at[CYCLES - 1, head], padded.at[0, tail], (down, other)),
    )
    return [
        pltpu.make_async_remote_copy(
            src_ref=src,
            dst_ref=dst,
            send_sem=send_sems.at[n],
            recv_sem=recv_sems.at[n],
            device_id=target,
            device_id_type=MESH,
        )
        for n, (src, dst, target) in enumerate(plan)
    ]


def partner(s, core):
    lat, lon = lax.axis_index("lat"), lax.axis_index("lon")
    x, z, y = lat >> 4, (lat >> 2) & 3, ((lat >> 1) & 1) + 2 * lon
    x, z, y = (x + (s >> 4)) & 3, (z + (s >> 2)) & 3, (y + s) & 3
    return (x << 4) + (z << 2) + ((y & 1) << 1) + ((lat + core) & 1), y >> 1


def for_partners(act):
    act(*partner(0, 1))

    def step(s, carry):
        far = (s * STRIDE) & (CHIPS - 1)
        act(*partner(far, 0))
        act(*partner(far, 1))
        return carry

    lax.fori_loop(1, CHIPS, step, 0)


def scatter(p, pick, received, send_sem, recv_sem):
    me = lax.axis_index("lat") * LONS + lax.axis_index("lon")

    def act(lat, lon):
        pltpu.make_async_remote_copy(
            src_ref=pick(lat, lon),
            dst_ref=received.at[p, me],
            send_sem=send_sem,
            recv_sem=recv_sem,
            device_id=(lat, lon),
            device_id_type=MESH,
        ).start()

    for_partners(act)


def arrival(p, received, send_sem, recv_sem):
    return pltpu.make_async_remote_copy(
        src_ref=received.at[p, pl.ds(0, DEVS - 1)],
        dst_ref=received.at[p, pl.ds(0, DEVS - 1)],
        send_sem=send_sem,
        recv_sem=recv_sem,
        device_id=partner(0, 1),
        device_id_type=MESH,
    )


def axis_peers():
    far = [16 * d for d in (1, 2, 3)] + [4 * d for d in (1, 2, 3)] + [1, 2, 3]
    return [partner(0, 1)] + [partner(d, 0) for d in far]


def signal_all(semaphore, peers):
    for peer in peers:
        pl.semaphore_signal(semaphore, inc=1, device_id=peer, device_id_type=MESH)


def kernel(
    taps, quad, field, mix_all, forward_all, inverse_all, legendre_all, weight_all, gain_all, conv,
    padded, band, terms, mix, forward, spectra, send, received,
    legendre, ones, table, turned, joined, coeffs, weight, gain, mixed,
    back, returned, inverse, synth,
    rounds, local_sems, halo_send, halo_recv, go_send, go_recv, back_send, back_recv,
):
    lat, lon = lax.axis_index("lat"), lax.axis_index("lon")
    me = lat * LONS + lon
    up, down, other = (lat + LATS - 1) % LATS, (lat + 1) % LATS, 1 - lon
    barrier = pltpu.get_barrier_semaphore()
    near = axis_peers()
    beside = [(up, lon), (down, lon), (up, other), (down, other)]
    signal_all(barrier, near + beside)
    loads = [
        pltpu.make_async_copy(src, dst, local_sems.at[n])
        for n, (src, dst) in enumerate(
            (
                (field, padded.at[pl.ds(1, CYCLES), pl.ds(EDGE, HALF)]),
                (mix_all, mix),
                (forward_all.at[lon], forward),
                (legendre_all.at[pl.ds(2 * lon, 2)], legendre),
                (weight_all, weight),
                (gain_all, gain),
                (inverse_all.at[lon], inverse),
            )
        )
    ]
    for load in loads:
        load.start()
    pl.semaphore_wait(barrier, len(near) + len(beside))
    copies = halo_copies(field, padded, halo_send, halo_recv)
    for copy in copies:
        copy.start()
    signal_all(rounds.at[0], near)
    loads[0].wait()
    build_taps(1, taps, band)
    basis_inner(1, padded, band, terms.at[0])
    pl.semaphore_wait(rounds.at[0], len(near))
    signal_all(rounds.at[1], near)
    for load in loads[1:]:
        load.wait()
    copies[0].wait_recv()
    copies[1].wait_recv()
    for s, i in enumerate(INNER):
        store = terms.at[s % 2]
        if s > 0:
            build_taps(i, taps, band)
            basis_inner(i, padded, band, store)
        basis_edges(i, padded, band, store)
        mix_terms(i, store, mix, conv)
        if s == 0:
            pl.semaphore_wait(rounds.at[1], len(near))
            signal_all(rounds.at[2], near)
        dft_cycle(s, i, quad, forward, conv, spectra)
    pack_inner(spectra, send)
    pl.semaphore_wait(rounds.at[2], len(near))

    def go(g):
        scatter(
            g, lambda a, b: send.at[g, a * LONS + b], received, go_send.at[g], go_recv.at[g]
        )
        received[g, me] = send[g, me]

    go(0)
    for copy in copies[2:]:
        copy.wait_recv()

    @pl.when(lat == 0)
    def _():
        padded[0] = jnp.zeros((WIDE, C), BF16)

    @pl.when(lat == LATS - 1)
    def _():
        padded[CYCLES + 1] = jnp.zeros((WIDE, C), BF16)

    for s, i in enumerate(OUTER):
        store = terms.at[s]
        build_taps(i, taps, band)
        basis_inner(i, padded, band, store)
        basis_edges(i, padded, band, store)
        mix_terms(i, store, mix, conv)
        dft_cycle(s, i, quad, forward, conv, spectra)
    pack_outer(spectra, send)
    go(1)
    go(2)
    build_triangle(4 * lat + 2 * lon, legendre, ones, table, turned)

    def take(g):
        arrival(g, received, go_send.at[g], go_recv.at[g]).wait_recv()
        legendre_group(g, received, joined, table, coeffs)

    def give(g):
        synth_group(g, turned, mixed, back)
        scatter(g, lambda a, b: back.at[g, a], returned, back_send.at[g], back_recv.at[g])
        returned[g, me] = back[g, lat]

    take(0)
    take(1)
    mix_modes(0, coeffs, weight, gain, mixed)
    give(0)
    take(2)
    mix_modes(1, coeffs, weight, gain, mixed)
    give(2)
    give(1)
    for g in (0, 2):
        arrival(g, returned, back_send.at[g], back_recv.at[g]).wait_recv()
    unpack_inner(returned, synth)
    for s, i in enumerate(INNER):
        inverse_cycle(s, i, inverse, synth, conv)
    arrival(1, returned, back_send.at[1], back_recv.at[1]).wait_recv()
    unpack_outer(returned, synth)
    for s, i in enumerate(OUTER):
        inverse_cycle(s, i, inverse, synth, conv)
    for copy in copies:
        copy.wait_send()
    for p in range(3):
        arrival(p, received, go_send.at[p], go_recv.at[p]).wait_send()
        arrival(p, returned, back_send.at[p], back_recv.at[p]).wait_send()


SMEM = pl.BlockSpec(memory_space=pltpu.SMEM)
VMEM = pl.BlockSpec(memory_space=pltpu.VMEM)
ANY = pl.BlockSpec(memory_space=pl.ANY)
LIMIT = 59 * 2**20


def body(grid_field, disco_taps, disco_mix, legendre, quad_weights, mix_weight, degree_gain):
    forward_all, inverse_all = dft_constants()
    dma = pltpu.SemaphoreType.DMA
    return pl.pallas_call(
        kernel,
        out_shape=pltpu.VMEM((CYCLES, HALF, C), BF16),
        in_specs=[SMEM, SMEM] + [ANY] * 7,
        out_specs=VMEM,
        scratch_shapes=[
            pltpu.VMEM((CYCLES + 2, WIDE, C), BF16),
            pltpu.VMEM((KERNELS * TILE, 3 * WINDOW), BF16),
            pltpu.VMEM((2, HALF, KERNELS * C), BF16),
            pltpu.VMEM((KERNELS * C, C), BF16),
            pltpu.VMEM((2 * MODES, HALF), BF16),
            pltpu.VMEM((4, 2 * MODES, C), F32),
            pltpu.VMEM((3, DEVS, 8, C), BF16),
            pltpu.VMEM((3, DEVS, 8, C), BF16),
            pltpu.VMEM((2, DEGREES, LATS * CYCLES), BF16),
            pltpu.VMEM((LATS * CYCLES, LATS * 8), BF16),
            pltpu.VMEM((3, 4 * DEGREES, LATS * 8), BF16),
            pltpu.VMEM((3, LATS * 8, 4 * DEGREES), BF16),
            pltpu.VMEM((LATS * 8, C), BF16),
            pltpu.VMEM((4 * DEGREES, C), F32),
            pltpu.VMEM((2, C, C), BF16),
            pltpu.VMEM((DEGREES, C), F32),
            pltpu.VMEM((4 * DEGREES, C), BF16),
            pltpu.VMEM((3, LATS, 8, C), BF16),
            pltpu.VMEM((3, DEVS, 8, C), BF16),
            pltpu.VMEM((HALF, 2 * MODES), BF16),
            pltpu.VMEM((4, 2 * MODES, C), BF16),
            pltpu.SemaphoreType.REGULAR((3,)),
            dma((7,)),
            dma((8,)),
            dma((8,)),
            dma((3,)),
            dma((3,)),
            dma((3,)),
            dma((3,)),
        ],
        compiler_params=pltpu.CompilerParams(
            collective_id=0, has_side_effects=True, vmem_limit_bytes=LIMIT
        ),
    )(
        disco_taps.transpose(0, 3, 2, 1),
        quad_weights,
        grid_field,
        disco_mix,
        forward_all,
        inverse_all,
        legendre,
        mix_weight,
        degree_gain,
    )


def solution(mesh):
    return jax.shard_map(
        body,
        mesh=mesh,
        in_specs=(
            P("lat", "lon", None),
            P(None, "lat", None, None),
            P(),
            P("lat", None, None),
            P("lat"),
            P(),
            P(),
        ),
        out_specs=P("lat", "lon", None),
        check_vma=False,
    )
```
